32 devices in a mesh: section: 4 (over z), expert: 8 (over y, x, core).
Axes of the slice: x: 2, y: 2, z: 4, core: 2. Of those that a mesh axis runs over, the one named last changes fastest.
Arguments:
- x_saved: bfloat16 [4, 8, 128, 2560], P('section', None, 'expert'), may hold values from -6 to 6
- routes: int32 [4, 8, 128, 2], P('section', None, 'expert'), may hold values from 0 to 3, all different within a row; in each aligned block of 16 rows (0 to 15, 16 to 31, ..., all dimensions but the last counted through in order) at most 12 rows name the same one
- gates: float32 [4, 8, 128, 2], P('section', None, 'expert'), may hold values from 0.1 to 0.6
- cotangent: bfloat16 [8, 128, 2560], P(None, 'expert', 'section'), may hold values from -6 to 6
- w_gate: bfloat16 [4, 3072, 2560], P('section', 'expert'), may hold values from -0.125 to 0.125
- w_up: bfloat16 [4, 3072, 2560], P('section', 'expert'), may hold values from -0.125 to 0.125
- w_down: bfloat16 [4, 3072, 2560], P('section', 'expert'), may hold values from -0.21875 to 0.21875
Outputs:
- grad_inputs: bfloat16 [4, 8, 128, 2560], P('section', None, 'expert')
- grad_gate: bfloat16 [4, 3072, 2560], P('section', 'expert')
- grad_up: bfloat16 [4, 3072, 2560], P('section', 'expert')
- grad_down: bfloat16 [4, 3072, 2560], P('section', 'expert')
The draws below stay inside these ranges and needn't reach their ends.
Inputs may be any that keep to these rules, and one draw needn't show every extreme that they name: `routes`: each token names 2 different experts. In each aligned block of 16 tokens (one device's tokens of one section and micro-batch), no expert is named by more than 12 tokens, and in some blocks one is named by exactly 12.
All inputs are finite; a program needn't handle non-finite values.
Results may differ from the reference program's by a relative error of at most 0.025.
Values may be sent and summed in bfloat16 or wider, within the bound.
A program may use at most 128 MiB of HBM per device.

```python
import math
import jax
import jax.numpy as jnp
import numpy as np
from jax import lax

D = 2560
FF = 768
SPLIT = 2
TOP = 2
MB = 8
TOK_DEV = 16
SECTIONS = 4
EXP_SECTION = 4
FF_DEV = 384
CAP = 12
TOKENS = 128
N_EXPERT = 8


def steps_of(stream_key, shape, shards, smallest, top_value):
    factor_of = 1.0
    for dim, shards_of in shards:
        steps = jax.random.uniform(jax.random.fold_in(jax.random.fold_in(stream_key, 6), dim), (shards_of,), jnp.float32, smallest / len(shards), top_value / len(shards))
        factor_of = factor_of * jnp.repeat(jnp.exp(steps), shape[dim] // shards_of).reshape((-1,) + (1,) * (len(shape) - 1 - dim))
    return factor_of


def shared_out(own_key, own, number, rows, number_of, top, most, lean):
    sequence = jax.random.permutation(own_key, number_of)
    heavy_load, usual = load_shares(number_of, rows * top, most, lean, True), load_shares(number_of, rows * top, most, lean, False)
    places = jnp.arange(number_of)

    def named(lengths, offset_by):
        used = int((lengths > 0).sum())
        fixed = max(1, used // 4)
        passed = fixed + (places - fixed + offset_by * (used - fixed)) % max(1, number_of - fixed)
        return jnp.zeros((number_of,), jnp.int32).at[sequence[jnp.where(places < fixed, places, passed)]].set(jnp.asarray(lengths, jnp.int32))

    lengths = jnp.where(number % 4 == 0, named(heavy_load, number // 4), named(usual, number - number // 4 - 1))
    mixed = jax.random.permutation(jax.random.fold_in(own, 3), number_of)
    donor, taker = mixed[0:number_of // 2 * 2:2], mixed[1:number_of // 2 * 2:2]
    margin = jnp.minimum(lengths[donor] - 1, most - lengths[taker]) // 2
    margin = jnp.where((donor == sequence[0]) | (taker == sequence[0]) | (lengths[taker] == 0), 0, jnp.maximum(margin, 0))
    passed = jax.random.randint(jax.random.fold_in(own, 4), (number_of // 2,), 0, 1 << 20) % (margin + 1)
    lengths = lengths.at[donor].add(-passed).at[taker].add(passed)
    members = jnp.searchsorted(jnp.cumsum(lengths), jnp.arange(rows * top), side="right").astype(jnp.int32)
    table = members.reshape(top, rows).T
    table = table[jax.random.permutation(jax.random.fold_in(own, 1), rows)]
    offset_by = jax.random.randint(jax.random.fold_in(own, 2), (rows, 1), 0, top)
    return jnp.take_along_axis(table, (jnp.arange(top)[None, :] + offset_by) % top, axis=1)


def load_shares(amount, total, bound, lean, full):
    weights = [(1 << 20) // math.isqrt(standing ** lean) + 1 for standing in range(1, amount + 1)]
    largest = bound if full else min(bound, max(-(-total // amount), total * weights[0] // sum(weights)))
    least = 1 if total - largest >= amount - 1 else 0
    given, surplus = [largest] + [least] * (amount - 1), total - largest - least * (amount - 1)
    while surplus > 0:
        candidates = [i for i in range(1, amount) if given[i] < largest] or [i for i in range(1, amount) if given[i] < bound]
        pool, left = sum([weights[i] for i in candidates]), surplus
        for i in candidates:
            extra = min(bound - given[i], max(1, left * weights[i] // pool), surplus)
            given[i] = given[i] + extra
            surplus = surplus - extra
    return np.array(given)


def gaussian(key, dims, scale, bound, shards=(), held_as=jnp.bfloat16):
    loudness = steps_of(key, dims, shards, -0.22, 0.18) if shards else 1.0
    values = jax.random.normal(key, dims, jnp.float32) * scale * loudness
    return jnp.minimum(jnp.maximum(values, -bound), bound).astype(held_as)


def setup_inputs(seed: int = 0) -> dict:
    key_list = jax.random.split(jax.random.key(seed), 8)
    x_saved = gaussian(key_list[0], (SECTIONS, MB, TOKENS, D), 1.0, 6.0, ((0, 4), (2, 8)))
    routes_keys = jax.random.split(jax.random.fold_in(key_list[1], 1), SECTIONS * MB * TOKENS // TOK_DEV)
    routes_turns = jax.random.permutation(jax.random.fold_in(key_list[1], 3), SECTIONS * MB * TOKENS // TOK_DEV)
    routes = jax.vmap(lambda own, number: shared_out(jax.random.fold_in(key_list[1], 2), own, number, TOK_DEV, EXP_SECTION, TOP, CAP, 2))(routes_keys, routes_turns).reshape((SECTIONS, MB, TOKENS, TOP))
    gates = jnp.clip(0.1 + 0.5 * jax.random.uniform(key_list[2], (SECTIONS, MB, TOKENS, TOP), jnp.float32) ** steps_of(key_list[2], (SECTIONS, MB, TOKENS, TOP), ((0, 4), (2, 8)), -0.2, 0.2), 0.1, 0.6)
    cotangent = gaussian(key_list[3], (MB, TOKENS, D), 1.0, 6.0, ((1, 8), (2, 4)))
    w_gate = gaussian(key_list[4], (SECTIONS, EXP_SECTION * FF, D), D ** -0.5, 0.125, ((0, 4), (1, 8)))
    w_up = gaussian(key_list[5], (SECTIONS, EXP_SECTION * FF, D), D ** -0.5, 0.125, ((0, 4), (1, 8)))
    w_down = gaussian(key_list[6], (SECTIONS, EXP_SECTION * FF, D), FF ** -0.5, 0.21875, ((0, 4), (1, 8)))
    return {"x_saved": x_saved, "routes": routes, "gates": gates, "cotangent": cotangent, "w_gate": w_gate, "w_up": w_up, "w_down": w_down}


def swish_parts(pre_gate):
    sigmoid = jax.nn.sigmoid(pre_gate)
    return pre_gate * sigmoid, sigmoid * (1.0 + pre_gate * (1.0 - sigmoid))


def expert_rows(operands):
    rows_in, rows_grad, gate_block, up_block, down_block = operands
    row_count = rows_in.shape[0]
    pre_gate = jnp.dot(rows_in, gate_block.T, preferred_element_type=jnp.float32)
    pre_up = jnp.dot(rows_in, up_block.T, preferred_element_type=jnp.float32)
    swished, slope_act = swish_parts(pre_gate)
    hidden_act = (swished * pre_up).astype(jnp.bfloat16)
    d_hidden = jnp.dot(rows_grad, down_block.T, preferred_element_type=jnp.float32)
    d_gate = (d_hidden * pre_up * slope_act).astype(jnp.bfloat16)
    d_up = (d_hidden * swished).astype(jnp.bfloat16)
    sliced_gate = d_gate.reshape(row_count, SPLIT, FF_DEV).astype(jnp.float32)
    sliced_up = d_up.reshape(row_count, SPLIT, FF_DEV).astype(jnp.float32)
    gate_parts = gate_block.reshape(SPLIT, FF_DEV, D).astype(jnp.float32)
    up_parts = up_block.reshape(SPLIT, FF_DEV, D).astype(jnp.float32)
    slice_part = jnp.einsum("rsf,sfd->srd", sliced_gate, gate_parts, precision=lax.Precision.HIGHEST)
    slice_part = slice_part + jnp.einsum("rsf,sfd->srd", sliced_up, up_parts, precision=lax.Precision.HIGHEST)
    rounded = lax.optimization_barrier(slice_part.astype(jnp.bfloat16))
    row_grad = jnp.sum(rounded.astype(jnp.float32), axis=0)
    gate_sum = jnp.dot(d_gate.T, rows_in, preferred_element_type=jnp.float32)
    up_sum = jnp.dot(d_up.T, rows_in, preferred_element_type=jnp.float32)
    down_sum = jnp.dot(hidden_act.T, rows_grad, preferred_element_type=jnp.float32)
    return row_grad, gate_sum, up_sum, down_sum


def section_batch(input_rows, route_rows, gate_values, upstream, gate_w, up_w, down_w):
    route_blocks = route_rows.reshape(N_EXPERT, TOK_DEV * TOP).astype(jnp.int32)
    route_hot = (route_blocks[:, :, None] == jnp.arange(EXP_SECTION, dtype=jnp.int32)[None, None, :]).astype(jnp.int32)
    earlier = jnp.cumsum(route_hot, axis=1) - route_hot
    position = jnp.sum(earlier * route_hot, axis=2)
    block_index = jnp.arange(N_EXPERT, dtype=jnp.int32)[:, None]
    target = (route_blocks * (N_EXPERT * CAP) + block_index * CAP + position).reshape(-1).astype(jnp.int32)
    slot_total = EXP_SECTION * N_EXPERT * CAP
    input_repeat = jnp.repeat(input_rows, TOP, axis=0)
    scaled = (jnp.repeat(upstream, TOP, axis=0).astype(jnp.float32) * gate_values.reshape(-1, 1)).astype(jnp.bfloat16)
    input_slots = jnp.zeros((slot_total, D), jnp.bfloat16).at[target].set(input_repeat)
    grad_slots = jnp.zeros((slot_total, D), jnp.bfloat16).at[target].set(scaled)
    operands = (input_slots.reshape(EXP_SECTION, N_EXPERT * CAP, D),
                grad_slots.reshape(EXP_SECTION, N_EXPERT * CAP, D),
                gate_w.reshape(EXP_SECTION, FF, D),
                up_w.reshape(EXP_SECTION, FF, D),
                down_w.reshape(EXP_SECTION, FF, D))
    row_grad, gate_sum, up_sum, down_sum = lax.map(expert_rows, operands)
    picked = row_grad.reshape(slot_total, D)[target]
    outgoing = (upstream.astype(jnp.float32) + jnp.sum(picked.reshape(TOKENS, TOP, D), axis=1)).astype(jnp.bfloat16)
    return outgoing, (gate_sum.reshape(EXP_SECTION * FF, D), up_sum.reshape(EXP_SECTION * FF, D), down_sum.reshape(EXP_SECTION * FF, D))


def reference(x_saved, routes, gates, cotangent, w_gate, w_up, w_down):
    def one_section(upstream_all, section_inputs):
        input_section, route_section, gate_section, gate_w, up_w, down_w = section_inputs

        def one_batch(running, batch_inputs):
            input_rows, route_rows, gate_values, upstream = batch_inputs
            outgoing, batch_sums = section_batch(input_rows, route_rows, gate_values, upstream, gate_w, up_w, down_w)
            return tuple(earlier_sum + batch_sum for earlier_sum, batch_sum in zip(running, batch_sums)), outgoing

        zero_grad = jnp.zeros((EXP_SECTION * FF, D), jnp.float32)
        running, outgoing_all = lax.scan(one_batch, (zero_grad, zero_grad, zero_grad), (input_section, route_section, gate_section, upstream_all))
        grads = tuple((running_sum / MB).astype(jnp.bfloat16) for running_sum in running)
        return outgoing_all, (outgoing_all,) + grads

    unused, stacked = lax.scan(one_section, cotangent, (x_saved, routes, gates, w_gate, w_up, w_down), reverse=True)
    return stacked[0], stacked[1], stacked[2], stacked[3]
```

```python
import functools

import jax
import jax.numpy as jnp
from jax import lax
from jax.experimental import pallas as pl
from jax.experimental.pallas import tpu as pltpu
from jax.sharding import PartitionSpec as P

SPLIT = 2
MESH = pl.DeviceIdType.MESH
COLS = (((1,), (1,)), ((), ()))
F32 = jnp.float32
BF16 = jnp.bfloat16


def relay_kernel(
    sections, experts, batches, groups, blk, tile,
    x_ref, cot_ref, gates_ref, place_ref, place_x_ref, place_t_ref, wg_ref, wu_ref, wd_ref,
    out_ref, dwg_ref, dwu_ref, dwd_ref,
    up_buf, x_send, x_rows, g_send, g_rows, r_send, r_recv, w_other, acts, acts_send, acts_t,
    slope_buf, swish_buf,
    x_ss, x_rs, g_ss, g_rs, r_ss, r_rs, hop_ss, hop_rs, top_ss, top_rs, w_ss, w_rs,
    px_ss, px_rs, pg_ss, pg_rs, pa_ss, pa_rs,
):
    section = lax.axis_index("section")
    place_in = lax.axis_index("expert")
    chip = place_in // SPLIT
    core = place_in % SPLIT
    other = chip * SPLIT + (1 - core)
    last = section == sections - 1
    rows = experts * blk
    width = x_ref.shape[2]
    hidden = wg_ref.shape[0]
    piece = cot_ref.shape[2]
    gathered = piece == width

    def remote(src, dst, ss, rs, sec, exp):
        return pltpu.make_async_remote_copy(
            src_ref=src, dst_ref=dst, send_sem=ss, recv_sem=rs,
            device_id=(sec, exp), device_id_type=MESH,
        )

    def peer(step):
        return lax.rem(chip + step, experts)

    barrier = pltpu.get_barrier_semaphore()
    for step in range(1, experts):
        pl.semaphore_signal(
            barrier, inc=1, device_id=(section, peer(step) * SPLIT + core), device_id_type=MESH
        )
    pl.semaphore_signal(barrier, inc=1, device_id=(section, other), device_id_type=MESH)
    for step in range(1, sections):
        pl.semaphore_signal(
            barrier, inc=1, device_id=(lax.rem(section + step, sections), place_in),
            device_id_type=MESH,
        )
    pl.semaphore_wait(barrier, experts - 1 + 1 + sections - 1)

    def exchange(send, recv, ss, rs, g, step):
        to = peer(step)
        return remote(
            send.at[g, to], recv.at[g, chip], ss.at[g, to], rs.at[g, chip],
            section, to * SPLIT + core,
        )

    def arrival(send, recv, ss, rs, g, step):
        source = peer(step)
        return remote(
            send.at[g, source], recv.at[g, source], ss.at[g, source], rs.at[g, source],
            section, source * SPLIT + core,
        )

    def send_all(send, recv, ss, rs, g):
        for step in range(1, experts):
            exchange(send, recv, ss, rs, g, step).start()

    def wait_all(send, recv, ss, rs, g):
        for step in range(1, experts):
            arrival(send, recv, ss, rs, g, step).wait_recv()

    def wait_sent(send, recv, ss, rs, g):
        for step in range(1, experts):
            exchange(send, recv, ss, rs, g, step).wait_send()

    def top_copy(g):
        return remote(
            cot_ref.at[g], up_buf.at[g, :, pl.ds(pl.multiple_of(section * piece, 128), piece)],
            top_ss.at[g], top_rs.at[g, section], sections - 1, place_in,
        )

    def hop_copy(g):
        return remote(
            out_ref.at[g], up_buf.at[g], hop_ss.at[g], hop_rs.at[g],
            jnp.maximum(section - 1, 0), place_in,
        )

    def to_partner(buf, ss, rs, g):
        return remote(buf.at[0, g], buf.at[1, g], ss.at[g], rs.at[g], section, other)

    def acts_copy(g):
        return remote(
            acts_send.at[g], acts.at[1, g], pa_ss.at[g], pa_rs.at[g], section, other
        )

    own_w = (wg_ref, wu_ref, wd_ref)
    weight_copies = [
        remote(own_w[i], w_other.at[i], w_ss.at[i], w_rs.at[i], section, other) for i in range(3)
    ]

    @pl.loop(0, groups)
    def _(g):
        if not gathered:
            @pl.when(jnp.logical_not(last))
            def _():
                top_copy(g).start()

        placed = jnp.dot(place_x_ref[g], x_ref[g], preferred_element_type=F32).astype(BF16)
        x_send[g] = placed.reshape(experts, blk, width)
        send_all(x_send, x_rows.at[0], x_ss, x_rs, g)
        x_rows[0, g, chip] = x_send[g, chip]

    for copy in weight_copies:
        copy.start()
    for copy in weight_copies:
        copy.wait_recv()

    def weights(which, half):
        return own_w[which] if half == 0 else w_other.at[which]

    def forward(g):
        wait_all(x_send, x_rows.at[0], x_ss, x_rs, g)
        to_partner(x_rows, px_ss, px_rs, g).start()
        rows_in = x_rows[0, g].reshape(rows, width)
        slot = lax.rem(g, 2)
        for half in range(2):
            pre_gate = lax.dot_general(
                rows_in, weights(0, half)[...], COLS, preferred_element_type=F32
            )
            pre_up = lax.dot_general(
                rows_in, weights(1, half)[...], COLS, preferred_element_type=F32
            )
            sigmoid = jax.nn.sigmoid(pre_gate)
            swished = pre_gate * sigmoid
            columns = pl.ds(half * hidden, hidden)
            swish_buf[slot, :, columns] = swished
            slope_buf[slot, :, columns] = pre_up * (sigmoid * (1.0 + pre_gate * (1.0 - sigmoid)))
            act = (swished * pre_up).astype(BF16)
            third = pl.ds(2 * hidden, hidden)
            if half == 0:
                acts[0, g, :, third] = act
            else:
                acts_send[g, :, third] = act

    forward(0)

    @pl.loop(0, groups)
    def _(g):
        @pl.when(last)
        def _():
            if gathered:
                up_buf[g] = cot_ref[g]
            else:
                for z in range(sections - 1):
                    remote(
                        cot_ref.at[g], up_buf.at[g, :, pl.ds(z * piece, piece)],
                        top_ss.at[g], top_rs.at[g, z], section, place_in,
                    ).wait_recv()
                up_buf[g, :, pl.ds((sections - 1) * piece, piece)] = cot_ref[g]

        @pl.when(jnp.logical_not(last))
        def _():
            hop_copy(g).wait_recv()

        upstream = up_buf[g].astype(F32)
        scaled = jnp.concatenate(
            [(upstream * gates_ref[g, k]).astype(BF16) for k in range(gates_ref.shape[1])], axis=0
        )
        placed = jnp.dot(place_ref[g], scaled, preferred_element_type=F32).astype(BF16)
        g_send[g] = placed.reshape(experts, blk, width)
        send_all(g_send, g_rows.at[0], g_ss, g_rs, g)
        g_rows[0, g, chip] = g_send[g, chip]

        @pl.when(g + 1 < groups)
        def _():
            forward(g + 1)

        wait_all(g_send, g_rows.at[0], g_ss, g_rs, g)
        to_partner(g_rows, pg_ss, pg_rs, g).start()
        rows_grad = g_rows[0, g].reshape(rows, width)
        slot = lax.rem(g, 2)
        slopes = []
        for half in range(2):
            d_hidden = lax.dot_general(
                rows_grad, weights(2, half)[...], COLS, preferred_element_type=F32
            )
            columns = pl.ds(half * hidden, hidden)
            d_gate = (d_hidden * slope_buf[slot, :, columns]).astype(BF16)
            d_up = (d_hidden * swish_buf[slot, :, columns]).astype(BF16)
            slopes.append((d_gate, d_up))
            if half == 0:
                acts[0, g, :, pl.ds(0, hidden)] = d_gate
                acts[0, g, :, pl.ds(hidden, hidden)] = d_up
            else:
                acts_send[g, :, pl.ds(0, hidden)] = d_gate
                acts_send[g, :, pl.ds(hidden, hidden)] = d_up

        @pl.loop(0, width // tile)
        def _(t):
            columns = pl.ds(pl.multiple_of(t * tile, 128), tile)
            total = jnp.zeros((rows, tile), F32)
            for half in range(2):
                for which in range(2):
                    total += jnp.dot(
                        slopes[half][which], weights(which, half)[:, columns],
                        preferred_element_type=F32,
                    )
            r_send[g, :, :, columns] = total.astype(BF16).reshape(experts, blk, tile)

        send_all(r_send, r_recv, r_ss, r_rs, g)
        r_recv[g, chip] = r_send[g, chip]
        acts_copy(g).start()
        wait_all(r_send, r_recv, r_ss, r_rs, g)
        back = jnp.dot(
            place_t_ref[g], r_recv[g].reshape(rows, width), preferred_element_type=F32
        )
        out_ref[g] = (up_buf[g].astype(F32) + back).astype(BF16)

        @pl.when(section > 0)
        def _():
            hop_copy(g).start()

    @pl.loop(0, groups)
    def _(g):
        to_partner(x_rows, px_ss, px_rs, g).wait_recv()
        to_partner(g_rows, pg_ss, pg_rs, g).wait_recv()
        acts_copy(g).wait_recv()

    total_rows = 2 * groups * rows
    for i in range(3):
        acts_t[pl.ds(i * hidden, hidden), :] = (
            acts[:, :, :, pl.ds(i * hidden, hidden)].reshape(total_rows, hidden).T
        )
    share = 1.0 / batches

    @pl.loop(0, width // 256)
    def _(t):
        columns = pl.ds(pl.multiple_of(t * 256, 128), 256)
        rows_in = x_rows[:, :, :, :, columns].reshape(total_rows, 256)
        rows_grad = g_rows[:, :, :, :, columns].reshape(total_rows, 256)
        for i, (result, side) in enumerate(
            ((dwg_ref, rows_in), (dwu_ref, rows_in), (dwd_ref, rows_grad))
        ):
            grad = jnp.dot(
                acts_t[pl.ds(i * hidden, hidden), :], side, preferred_element_type=F32
            )
            result[:, columns] = (grad * share).astype(BF16)

    @pl.loop(0, groups)
    def _(g):
        wait_sent(x_send, x_rows.at[0], x_ss, x_rs, g)
        wait_sent(g_send, g_rows.at[0], g_ss, g_rs, g)
        wait_sent(r_send, r_recv, r_ss, r_rs, g)
        to_partner(x_rows, px_ss, px_rs, g).wait_send()
        to_partner(g_rows, pg_ss, pg_rs, g).wait_send()
        acts_copy(g).wait_send()

        @pl.when(section > 0)
        def _():
            hop_copy(g).wait_send()

        if not gathered:
            @pl.when(jnp.logical_not(last))
            def _():
                top_copy(g).wait_send()

    for copy in weight_copies:
        copy.wait_send()


def on_device(group_rows, x_saved, routes, gates, cotangent, w_gate, w_up, w_down):
    sections = lax.axis_size("section")
    experts = lax.axis_size("expert") // SPLIT
    batches, tokens, width = x_saved.shape[1:]
    top = routes.shape[3]
    hidden = w_gate.shape[1]
    capacity = max(2, 3 * tokens * top // (2 * experts))
    per = 1
    while per * capacity < group_rows and batches % (2 * per) == 0:
        per *= 2
    groups = batches // per
    blk = -(-per * capacity // 16) * 16
    rows = experts * blk
    tile = 512 if width % 512 == 0 else 128

    flat = routes[0].reshape(batches, tokens * top)
    hot = (flat[:, :, None] == jnp.arange(experts, dtype=jnp.int32)).astype(jnp.int32)
    earlier = jnp.cumsum(hot, axis=1) - hot
    within = jnp.sum(earlier * hot, axis=2)
    batch_in = jnp.arange(batches, dtype=jnp.int32)[:, None] % per
    target = (flat * blk + batch_in * capacity + within).reshape(groups, per, tokens, top)
    target = jnp.transpose(target, (0, 3, 1, 2)).reshape(groups, top, per * tokens)
    spots = jnp.arange(rows, dtype=jnp.int32)
    place = (spots[None, :, None] == target.reshape(groups, 1, -1)).astype(BF16)
    place_x = jnp.any(spots[None, :, None, None] == target[:, None], axis=2).astype(BF16)
    place_t = jnp.any(target[:, :, :, None] == spots, axis=1).astype(BF16)
    scales = jnp.transpose(
        gates[0].reshape(groups, per * tokens, top), (0, 2, 1)
    )[..., None]
    x_groups = x_saved[0].reshape(groups, per * tokens, width)
    if cotangent.shape[2] % 128:
        cotangent = lax.all_gather(cotangent, "section", axis=2, tiled=True)
    cot_groups = cotangent.reshape(groups, per * tokens, cotangent.shape[2])

    vmem = pl.BlockSpec(memory_space=pltpu.VMEM)
    slots = (groups, experts, blk, width)
    dma = pltpu.SemaphoreType.DMA
    grad_w = jax.ShapeDtypeStruct((hidden, width), BF16)
    results = pl.pallas_call(
        functools.partial(relay_kernel, sections, experts, batches, groups, blk, tile),
        out_shape=(
            jax.ShapeDtypeStruct((groups, per * tokens, width), BF16), grad_w, grad_w, grad_w,
        ),
        in_specs=[vmem] * 9,
        out_specs=(vmem,) * 4,
        scratch_shapes=[
            pltpu.VMEM((groups, per * tokens, width), BF16),
            pltpu.VMEM(slots, BF16),
            pltpu.VMEM((2,) + slots, BF16),
            pltpu.VMEM(slots, BF16),
            pltpu.VMEM((2,) + slots, BF16),
            pltpu.VMEM(slots, BF16),
            pltpu.VMEM(slots, BF16),
            pltpu.VMEM((3, hidden, width), BF16),
            pltpu.VMEM((2, groups, rows, 3 * hidden), BF16),
            pltpu.VMEM((groups, rows, 3 * hidden), BF16),
            pltpu.VMEM((3 * hidden, 2 * groups * rows), BF16),
            pltpu.VMEM((2, rows, 2 * hidden), F32),
            pltpu.VMEM((2, rows, 2 * hidden), F32),
        ]
        + [dma((groups, experts))] * 6
        + [dma((groups,)), dma((groups,)), dma((groups,)), dma((groups, sections))]
        + [dma((3,))] * 2
        + [dma((groups,))] * 6,
        compiler_params=pltpu.CompilerParams(
            collective_id=0, has_side_effects=True, vmem_limit_bytes=60 * 2**20
        ),
    )(
        x_groups, cot_groups, scales, place, place_x, place_t, w_gate[0], w_up[0], w_down[0]
    )
    grad_inputs = results[0].reshape(1, batches, tokens, width)
    return (grad_inputs, results[1][None], results[2][None], results[3][None])


def solution(mesh):
    rows = P("section", None, "expert", None)
    halves = P("section", "expert", None)
    return jax.shard_map(
        functools.partial(on_device, 12), mesh=mesh,
        in_specs=(rows, rows, rows, P(None, "expert", "section"), halves, halves, halves),
        out_specs=(rows, halves, halves, halves),
        check_vma=False,
    )
```

```python
import functools

import jax
import jax.numpy as jnp
from jax import lax
from jax.experimental import pallas as pl
from jax.experimental.pallas import tpu as pltpu
from jax.sharding import PartitionSpec as P

SPLIT = 2
MESH = pl.DeviceIdType.MESH
COLS = (((1,), (1,)), ((), ()))
F32 = jnp.float32
BF16 = jnp.bfloat16


def relay_kernel(
    sections, experts, batches, groups, blk, tile,
    x_ref, cot_ref, gates_ref, place_ref, place_x_ref, place_t_ref, wg_ref, wu_ref, wd_ref,
    out_ref, dwg_ref, dwu_ref, dwd_ref,
    up_buf, x_send, x_rows, g_send, g_rows, r_send, r_recv, w_other, acts, acts_send, acts_t,
    slope_buf, swish_buf,
    x_ss, x_rs, g_ss, g_rs, r_ss, r_rs, hop_ss, hop_rs, top_ss, top_rs, w_ss, w_rs,
    px_ss, px_rs, pg_ss, pg_rs, pa_ss, pa_rs,
):
    section = lax.axis_index("section")
    place_in = lax.axis_index("expert")
    chip = place_in // SPLIT
    core = place_in % SPLIT
    other = chip * SPLIT + (1 - core)
    last = section == sections - 1
    rows = experts * blk
    width = x_ref.shape[2]
    hidden = wg_ref.shape[0]
    piece = cot_ref.shape[2]
    gathered = piece == width

    def remote(src, dst, ss, rs, sec, exp):
        return pltpu.make_async_remote_copy(
            src_ref=src, dst_ref=dst, send_sem=ss, recv_sem=rs,
            device_id=(sec, exp), device_id_type=MESH,
        )

    def peer(step):
        return lax.rem(chip + step, experts)

    barrier = pltpu.get_barrier_semaphore()
    for step in range(1, experts):
        pl.semaphore_signal(
            barrier, inc=1, device_id=(section, peer(step) * SPLIT + core), device_id_type=MESH
        )
    pl.semaphore_signal(barrier, inc=1, device_id=(section, other), device_id_type=MESH)
    for step in range(1, sections):
        pl.semaphore_signal(
            barrier, inc=1, device_id=(lax.rem(section + step, sections), place_in),
            device_id_type=MESH,
        )
    pl.semaphore_wait(barrier, experts - 1 + 1 + sections - 1)

    def exchange(send, recv, ss, rs, g, step):
        to = peer(step)
        return remote(
            send.at[g, to], recv.at[g, chip], ss.at[g, to], rs.at[g, chip],
            section, to * SPLIT + core,
        )

    def arrival(send, recv, ss, rs, g, step):
        source = peer(step)
        return remote(
            send.at[g, source], recv.at[g, source], ss.at[g, source], rs.at[g, source],
            section, source * SPLIT + core,
        )

    def send_all(send, recv, ss, rs, g):
        for step in range(1, experts):
            exchange(send, recv, ss, rs, g, step).start()

    def wait_all(send, recv, ss, rs, g):
        for step in range(1, experts):
            arrival(send, recv, ss, rs, g, step).wait_recv()

    def wait_sent(send, recv, ss, rs, g):
        for step in range(1, experts):
            exchange(send, recv, ss, rs, g, step).wait_send()

    def top_copy(g):
        return remote(
            cot_ref.at[g], up_buf.at[g, :, pl.ds(pl.multiple_of(section * piece, 128), piece)],
            top_ss.at[g], top_rs.at[g, section], sections - 1, place_in,
        )

    def hop_copy(g):
        return remote(
            out_ref.at[g], up_buf.at[g], hop_ss.at[g], hop_rs.at[g],
            jnp.maximum(section - 1, 0), place_in,
        )

    def to_partner(buf, ss, rs, g):
        return remote(buf.at[0, g], buf.at[1, g], ss.at[g], rs.at[g], section, other)

    def acts_copy(g):
        return remote(
            acts_send.at[g], acts.at[1, g], pa_ss.at[g], pa_rs.at[g], section, other
        )

    own_w = (wg_ref, wu_ref, wd_ref)
    weight_copies = [
        remote(own_w[i], w_other.at[i], w_ss.at[i], w_rs.at[i], section, other) for i in range(3)
    ]

    ahead = jnp.where(last, min(2, groups), groups)
    early = jnp.minimum(1 + 3 * (sections - 1 - section), groups)

    for copy in weight_copies:
        copy.start()

    @pl.loop(0, groups)
    def _(g):
        if not gathered:
            @pl.when(jnp.logical_not(last))
            def _():
                top_copy(g).start()

        placed = jnp.dot(place_x_ref[g], x_ref[g], preferred_element_type=F32).astype(BF16)
        x_send[g] = placed.reshape(experts, blk, width)

        @pl.when(g < ahead)
        def _():
            send_all(x_send, x_rows.at[0], x_ss, x_rs, g)

        x_rows[0, g, chip] = x_send[g, chip]

    def weights(which, half):
        return own_w[which] if half == 0 else w_other.at[which]

    def forward_half(g, half):
        rows_in = x_rows[0, g].reshape(rows, width)
        pre_gate = lax.dot_general(
            rows_in, weights(0, half)[...], COLS, preferred_element_type=F32
        )
        pre_up = lax.dot_general(
            rows_in, weights(1, half)[...], COLS, preferred_element_type=F32
        )
        sigmoid = jax.nn.sigmoid(pre_gate)
        swished = pre_gate * sigmoid
        columns = pl.ds(half * hidden, hidden)
        swish_buf[g, :, columns] = swished
        slope_buf[g, :, columns] = pre_up * (sigmoid * (1.0 + pre_gate * (1.0 - sigmoid)))
        act = (swished * pre_up).astype(BF16)
        third = pl.ds(2 * hidden, hidden)
        if half == 0:
            acts[0, g, :, third] = act
        else:
            acts_send[g, :, third] = act

    def rows_arrived(g):
        wait_all(x_send, x_rows.at[0], x_ss, x_rs, g)
        to_partner(x_rows, px_ss, px_rs, g).start()

    def forward(g):
        rows_arrived(g)
        for half in range(2):
            forward_half(g, half)

    def dispatch(g):
        @pl.when(last)
        def _():
            if gathered:
                up_buf[g] = cot_ref[g]
            else:
                for z in range(sections - 1):
                    remote(
                        cot_ref.at[g], up_buf.at[g, :, pl.ds(z * piece, piece)],
                        top_ss.at[g], top_rs.at[g, z], section, place_in,
                    ).wait_recv()
                up_buf[g, :, pl.ds((sections - 1) * piece, piece)] = cot_ref[g]

        @pl.when(jnp.logical_not(last))
        def _():
            hop_copy(g).wait_recv()

        upstream = up_buf[g].astype(F32)
        scaled = jnp.concatenate(
            [(upstream * gates_ref[g, k]).astype(BF16) for k in range(gates_ref.shape[1])], axis=0
        )
        placed = jnp.dot(place_ref[g], scaled, preferred_element_type=F32).astype(BF16)
        g_send[g] = placed.reshape(experts, blk, width)
        send_all(g_send, g_rows.at[0], g_ss, g_rs, g)
        g_rows[0, g, chip] = g_send[g, chip]

    def backward(g):
        wait_all(g_send, g_rows.at[0], g_ss, g_rs, g)
        rows_grad = g_rows[0, g].reshape(rows, width)
        slopes = []
        for half in range(2):
            d_hidden = lax.dot_general(
                rows_grad, weights(2, half)[...], COLS, preferred_element_type=F32
            )
            columns = pl.ds(half * hidden, hidden)
            d_gate = (d_hidden * slope_buf[g, :, columns]).astype(BF16)
            d_up = (d_hidden * swish_buf[g, :, columns]).astype(BF16)
            slopes.append((d_gate, d_up))
            if half == 0:
                acts[0, g, :, pl.ds(0, hidden)] = d_gate
                acts[0, g, :, pl.ds(hidden, hidden)] = d_up
            else:
                acts_send[g, :, pl.ds(0, hidden)] = d_gate
                acts_send[g, :, pl.ds(hidden, hidden)] = d_up

        @pl.loop(0, width // tile)
        def _(t):
            columns = pl.ds(pl.multiple_of(t * tile, 128), tile)
            total = jnp.zeros((rows, tile), F32)
            for half in range(2):
                for which in range(2):
                    total += jnp.dot(
                        slopes[half][which], weights(which, half)[:, columns],
                        preferred_element_type=F32,
                    )
            r_send[g, :, :, columns] = total.astype(BF16).reshape(experts, blk, tile)

        send_all(r_send, r_recv, r_ss, r_rs, g)
        r_recv[g, chip] = r_send[g, chip]
        to_partner(g_rows, pg_ss, pg_rs, g).start()
        acts_copy(g).start()

    def combine(g):
        wait_all(r_send, r_recv, r_ss, r_rs, g)
        back = jnp.dot(
            place_t_ref[g], r_recv[g].reshape(rows, width), preferred_element_type=F32
        )
        out_ref[g] = (up_buf[g].astype(F32) + back).astype(BF16)

        @pl.when(section > 0)
        def _():
            hop_copy(g).start()

    rows_arrived(0)
    forward_half(0, 0)
    weight_copies[0].wait_recv()
    weight_copies[1].wait_recv()
    forward_half(0, 1)

    @pl.loop(1, early)
    def _(g):
        forward(g)

    weight_copies[2].wait_recv()

    @pl.loop(0, groups + 1)
    def _(g):
        @pl.when(g < groups)
        def _():
            dispatch(g)

        @pl.when(jnp.logical_and(last, g + 2 < groups))
        def _():
            send_all(x_send, x_rows.at[0], x_ss, x_rs, g + 2)

        @pl.when(jnp.logical_and(g + 1 >= early, g + 1 < groups))
        def _():
            forward(g + 1)

        @pl.when(g > 0)
        def _():
            combine(g - 1)

        @pl.when(g < groups)
        def _():
            backward(g)

    @pl.loop(0, groups)
    def _(g):
        to_partner(x_rows, px_ss, px_rs, g).wait_recv()
        to_partner(g_rows, pg_ss, pg_rs, g).wait_recv()
        acts_copy(g).wait_recv()

    total_rows = 2 * groups * rows
    for i in range(3):
        acts_t[pl.ds(i * hidden, hidden), :] = (
            acts[:, :, :, pl.ds(i * hidden, hidden)].reshape(total_rows, hidden).T
        )
    share = 1.0 / batches

    @pl.loop(0, width // 256)
    def _(t):
        columns = pl.ds(pl.multiple_of(t * 256, 128), 256)
        rows_in = x_rows[:, :, :, :, columns].reshape(total_rows, 256)
        rows_grad = g_rows[:, :, :, :, columns].reshape(total_rows, 256)
        for i, (result, side) in enumerate(
            ((dwg_ref, rows_in), (dwu_ref, rows_in), (dwd_ref, rows_grad))
        ):
            grad = jnp.dot(
                acts_t[pl.ds(i * hidden, hidden), :], side, preferred_element_type=F32
            )
            result[:, columns] = (grad * share).astype(BF16)

    @pl.loop(0, groups)
    def _(g):
        wait_sent(x_send, x_rows.at[0], x_ss, x_rs, g)
        wait_sent(g_send, g_rows.at[0], g_ss, g_rs, g)
        wait_sent(r_send, r_recv, r_ss, r_rs, g)
        to_partner(x_rows, px_ss, px_rs, g).wait_send()
        to_partner(g_rows, pg_ss, pg_rs, g).wait_send()
        acts_copy(g).wait_send()

        @pl.when(section > 0)
        def _():
            hop_copy(g).wait_send()

        if not gathered:
            @pl.when(jnp.logical_not(last))
            def _():
                top_copy(g).wait_send()

    for copy in weight_copies:
        copy.wait_send()


def on_device(group_rows, x_saved, routes, gates, cotangent, w_gate, w_up, w_down):
    sections = lax.axis_size("section")
    experts = lax.axis_size("expert") // SPLIT
    batches, tokens, width = x_saved.shape[1:]
    top = routes.shape[3]
    hidden = w_gate.shape[1]
    capacity = max(2, 3 * tokens * top // (2 * experts))
    per = 1
    while per * capacity < group_rows and batches % (2 * per) == 0:
        per *= 2
    groups = batches // per
    blk = -(-per * capacity // 16) * 16
    rows = experts * blk
    tile = 512 if width % 512 == 0 else 128

    flat = routes[0].reshape(batches, tokens * top)
    hot = (flat[:, :, None] == jnp.arange(experts, dtype=jnp.int32)).astype(jnp.int32)
    earlier = jnp.cumsum(hot, axis=1) - hot
    within = jnp.sum(earlier * hot, axis=2)
    batch_in = jnp.arange(batches, dtype=jnp.int32)[:, None] % per
    target = (flat * blk + batch_in * capacity + within).reshape(groups, per, tokens, top)
    target = jnp.transpose(target, (0, 3, 1, 2)).reshape(groups, top, per * tokens)
    spots = jnp.arange(rows, dtype=jnp.int32)
    place = (spots[None, :, None] == target.reshape(groups, 1, -1)).astype(BF16)
    place_x = jnp.any(spots[None, :, None, None] == target[:, None], axis=2).astype(BF16)
    place_t = jnp.any(target[:, :, :, None] == spots, axis=1).astype(BF16)
    scales = jnp.transpose(
        gates[0].reshape(groups, per * tokens, top), (0, 2, 1)
    )[..., None]
    x_groups = x_saved[0].reshape(groups, per * tokens, width)
    if cotangent.shape[2] % 128:
        cotangent = lax.all_gather(cotangent, "section", axis=2, tiled=True)
    cot_groups = cotangent.reshape(groups, per * tokens, cotangent.shape[2])

    vmem = pl.BlockSpec(memory_space=pltpu.VMEM)
    slots = (groups, experts, blk, width)
    dma = pltpu.SemaphoreType.DMA
    grad_w = jax.ShapeDtypeStruct((hidden, width), BF16)
    results = pl.pallas_call(
        functools.partial(relay_kernel, sections, experts, batches, groups, blk, tile),
        out_shape=(
            jax.ShapeDtypeStruct((groups, per * tokens, width), BF16), grad_w, grad_w, grad_w,
        ),
        in_specs=[vmem] * 9,
        out_specs=(vmem,) * 4,
        scratch_shapes=[
            pltpu.VMEM((groups, per * tokens, width), BF16),
            pltpu.VMEM(slots, BF16),
            pltpu.VMEM((2,) + slots, BF16),
            pltpu.VMEM(slots, BF16),
            pltpu.VMEM((2,) + slots, BF16),
            pltpu.VMEM(slots, BF16),
            pltpu.VMEM(slots, BF16),
            pltpu.VMEM((3, hidden, width), BF16),
            pltpu.VMEM((2, groups, rows, 3 * hidden), BF16),
            pltpu.VMEM((groups, rows, 3 * hidden), BF16),
            pltpu.VMEM((3 * hidden, 2 * groups * rows), BF16),
            pltpu.VMEM((groups, rows, 2 * hidden), F32),
            pltpu.VMEM((groups, rows, 2 * hidden), F32),
        ]
        + [dma((groups, experts))] * 6
        + [dma((groups,)), dma((groups,)), dma((groups,)), dma((groups, sections))]
        + [dma((3,))] * 2
        + [dma((groups,))] * 6,
        compiler_params=pltpu.CompilerParams(
            collective_id=0, has_side_effects=True, vmem_limit_bytes=60 * 2**20
        ),
    )(
        x_groups, cot_groups, scales, place, place_x, place_t, w_gate[0], w_up[0], w_down[0]
    )
    grad_inputs = results[0].reshape(1, batches, tokens, width)
    return (grad_inputs, results[1][None], results[2][None], results[3][None])


def solution(mesh):
    rows = P("section", None, "expert", None)
    halves = P("section", "expert", None)
    return jax.shard_map(
        functools.partial(on_device, 12), mesh=mesh,
        in_specs=(rows, rows, rows, P(None, "expert", "section"), halves, halves, halves),
        out_specs=(rows, halves, halves, halves),
        check_vma=False,
    )
```

```python
import functools

import jax
import jax.numpy as jnp
from jax import lax
from jax.experimental import pallas as pl
from jax.experimental.pallas import tpu as pltpu
from jax.sharding import PartitionSpec as P

SPLIT = 2
MESH = pl.DeviceIdType.MESH
COLS = (((1,), (1,)), ((), ()))
F32 = jnp.float32
BF16 = jnp.bfloat16


def relay_kernel(
    sections, experts, batches, groups, pair, blk, tile,
    x_ref, cot_ref, gates_ref, place_ref, place_x_ref, place_t_ref, wg_ref, wu_ref, wd_ref,
    out_ref, dwg_ref, dwu_ref, dwd_ref,
    up_buf, x_send, x_rows, g_send, g_rows, r_send, r_recv, w_gu, w_d, acts, acts_send, acts_t,
    slope_buf, swish_buf,
    x_ss, x_rs, g_ss, g_rs, r_ss, r_rs, hop_ss, hop_rs, top_ss, top_rs, w_ss, w_rs, w_ls,
    px_ss, px_rs, pg_ss, pg_rs, pa_ss, pa_rs,
):
    section = lax.axis_index("section")
    place_in = lax.axis_index("expert")
    chip = place_in // SPLIT
    core = place_in % SPLIT
    other = chip * SPLIT + (1 - core)
    last = section == sections - 1
    rows = experts * blk
    width = x_ref.shape[2]
    hidden = wg_ref.shape[0]
    piece = cot_ref.shape[2]
    gathered = piece == width

    def remote(src, dst, ss, rs, sec, exp):
        return pltpu.make_async_remote_copy(
            src_ref=src, dst_ref=dst, send_sem=ss, recv_sem=rs,
            device_id=(sec, exp), device_id_type=MESH,
        )

    def peer(step):
        return lax.rem(chip + step, experts)

    own_w = (wg_ref, wu_ref, wd_ref)
    own_at = [w_gu.at[pl.ds(0, hidden)], w_gu.at[pl.ds(hidden, hidden)], w_d.at[pl.ds(0, hidden)]]
    other_at = [
        w_gu.at[pl.ds(2 * hidden, hidden)], w_gu.at[pl.ds(3 * hidden, hidden)],
        w_d.at[pl.ds(hidden, hidden)],
    ]
    local_copies = [
        pltpu.make_async_copy(own_w[i], own_at[i], w_ls.at[i]) for i in range(3)
    ]
    for copy in local_copies:
        copy.start()

    barrier = pltpu.get_barrier_semaphore()
    for step in range(1, experts):
        pl.semaphore_signal(
            barrier, inc=1, device_id=(section, peer(step) * SPLIT + core), device_id_type=MESH
        )
    pl.semaphore_signal(barrier, inc=1, device_id=(section, other), device_id_type=MESH)
    for step in range(1, sections):
        pl.semaphore_signal(
            barrier, inc=1, device_id=(lax.rem(section + step, sections), place_in),
            device_id_type=MESH,
        )
    pl.semaphore_wait(barrier, experts - 1 + 1 + sections - 1)

    def exchange(send, recv, ss, rs, g, step):
        to = peer(step)
        return remote(
            send.at[g, to], recv.at[g, chip], ss.at[g, to], rs.at[g, chip],
            section, to * SPLIT + core,
        )

    def arrival(send, recv, ss, rs, g, step):
        source = peer(step)
        return remote(
            send.at[g, source], recv.at[g, source], ss.at[g, source], rs.at[g, source],
            section, source * SPLIT + core,
        )

    def send_all(send, recv, ss, rs, g):
        for step in range(1, experts):
            exchange(send, recv, ss, rs, g, step).start()

    def wait_all(send, recv, ss, rs, g):
        for step in range(1, experts):
            arrival(send, recv, ss, rs, g, step).wait_recv()

    def wait_sent(send, recv, ss, rs, g):
        for step in range(1, experts):
            exchange(send, recv, ss, rs, g, step).wait_send()

    def top_copy(g):
        return remote(
            cot_ref.at[g], up_buf.at[g, :, pl.ds(pl.multiple_of(section * piece, 128), piece)],
            top_ss.at[g], top_rs.at[g, section], sections - 1, place_in,
        )

    def hop_copy(g):
        return remote(
            out_ref.at[g], up_buf.at[g], hop_ss.at[g], hop_rs.at[g],
            jnp.maximum(section - 1, 0), place_in,
        )

    def to_partner(buf, ss, rs, g):
        return remote(buf.at[0, g], buf.at[1, g], ss.at[g], rs.at[g], section, other)

    def acts_copy(g):
        return remote(
            acts_send.at[g], acts.at[1, g], pa_ss.at[g], pa_rs.at[g], section, other
        )

    weight_copies = [
        remote(own_w[i], other_at[i], w_ss.at[i], w_rs.at[i], section, other) for i in range(3)
    ]

    ahead = jnp.where(last, min(pair, groups), groups)
    for copy in weight_copies:
        copy.start()

    @pl.loop(0, groups)
    def _(g):
        if not gathered:
            @pl.when(jnp.logical_not(last))
            def _():
                top_copy(g).start()

        placed = jnp.dot(place_x_ref[g], x_ref[g], preferred_element_type=F32).astype(BF16)
        x_send[g] = placed.reshape(experts, blk, width)

        @pl.when(g < ahead)
        def _():
            send_all(x_send, x_rows.at[0], x_ss, x_rs, g)

        x_rows[0, g, chip] = x_send[g, chip]

    def rows_arrived(g):
        wait_all(x_send, x_rows.at[0], x_ss, x_rs, g)
        to_partner(x_rows, px_ss, px_rs, g).start()

    def forward(p):
        first = p * pair
        for i in range(pair):
            rows_arrived(first + i)
        members = pl.ds(first, pair)
        rows_in = x_rows[0, members].reshape(pair * rows, width)
        for half in range(2):
            both = lax.dot_general(
                rows_in, w_gu[pl.ds(half * 2 * hidden, 2 * hidden), :], COLS,
                preferred_element_type=F32,
            )
            pre_gate, pre_up = both[:, :hidden], both[:, hidden:]
            sigmoid = jax.nn.sigmoid(pre_gate)
            swished = pre_gate * sigmoid
            slope = pre_up * (sigmoid * (1.0 + pre_gate * (1.0 - sigmoid)))
            act = (swished * pre_up).astype(BF16)
            columns = pl.ds(half * hidden, hidden)
            swish_buf[members, :, columns] = swished.reshape(pair, rows, hidden)
            slope_buf[members, :, columns] = slope.reshape(pair, rows, hidden)
            third = pl.ds(2 * hidden, hidden)
            if half == 0:
                acts[0, members, :, third] = act.reshape(pair, rows, hidden)
            else:
                acts_send[members, :, third] = act.reshape(pair, rows, hidden)

    def dispatch(g):
        @pl.when(last)
        def _():
            if gathered:
                up_buf[g] = cot_ref[g]
            else:
                for z in range(sections - 1):
                    remote(
                        cot_ref.at[g], up_buf.at[g, :, pl.ds(z * piece, piece)],
                        top_ss.at[g], top_rs.at[g, z], section, place_in,
                    ).wait_recv()
                up_buf[g, :, pl.ds((sections - 1) * piece, piece)] = cot_ref[g]

        @pl.when(jnp.logical_not(last))
        def _():
            hop_copy(g).wait_recv()

        upstream = up_buf[g].astype(F32)
        scaled = jnp.concatenate(
            [(upstream * gates_ref[g, k]).astype(BF16) for k in range(gates_ref.shape[1])], axis=0
        )
        placed = jnp.dot(place_ref[g], scaled, preferred_element_type=F32).astype(BF16)
        g_send[g] = placed.reshape(experts, blk, width)
        send_all(g_send, g_rows.at[0], g_ss, g_rs, g)
        g_rows[0, g, chip] = g_send[g, chip]

    def backward(g):
        wait_all(g_send, g_rows.at[0], g_ss, g_rs, g)
        rows_grad = g_rows[0, g].reshape(rows, width)
        d_hidden = lax.dot_general(rows_grad, w_d[...], COLS, preferred_element_type=F32)
        d_gate = (d_hidden * slope_buf[g]).astype(BF16)
        d_up = (d_hidden * swish_buf[g]).astype(BF16)
        slopes = jnp.concatenate(
            [d_gate[:, :hidden], d_up[:, :hidden], d_gate[:, hidden:], d_up[:, hidden:]], axis=1
        )
        acts[0, g, :, pl.ds(0, 2 * hidden)] = slopes[:, : 2 * hidden]
        acts_send[g, :, pl.ds(0, 2 * hidden)] = slopes[:, 2 * hidden :]

        @pl.loop(0, width // tile)
        def _(t):
            columns = pl.ds(pl.multiple_of(t * tile, 128), tile)
            total = jnp.dot(slopes, w_gu[:, columns], preferred_element_type=F32)
            r_send[g, :, :, columns] = total.astype(BF16).reshape(experts, blk, tile)

        send_all(r_send, r_recv, r_ss, r_rs, g)
        r_recv[g, chip] = r_send[g, chip]
        to_partner(g_rows, pg_ss, pg_rs, g).start()
        acts_copy(g).start()

    def combine(g):
        wait_all(r_send, r_recv, r_ss, r_rs, g)
        back = jnp.dot(
            place_t_ref[g], r_recv[g].reshape(rows, width), preferred_element_type=F32
        )
        out_ref[g] = (up_buf[g].astype(F32) + back).astype(BF16)

        @pl.when(section > 0)
        def _():
            hop_copy(g).start()

    for i in range(2):
        local_copies[i].wait()
        weight_copies[i].wait_recv()

    @pl.loop(0, jnp.where(last, 0, groups // pair))
    def _(p):
        forward(p)

    local_copies[2].wait()
    weight_copies[2].wait_recv()

    @pl.loop(0, groups + 1)
    def _(g):
        @pl.when(g < groups)
        def _():
            dispatch(g)

        @pl.when(jnp.logical_and(last, g + pair < groups))
        def _():
            send_all(x_send, x_rows.at[0], x_ss, x_rs, g + pair)

        @pl.when(jnp.logical_and(last, jnp.logical_and(g < groups, lax.rem(g, pair) == 0)))
        def _():
            forward(g // pair)

        @pl.when(g > 0)
        def _():
            combine(g - 1)

        @pl.when(g < groups)
        def _():
            backward(g)

    @pl.loop(0, groups)
    def _(g):
        to_partner(x_rows, px_ss, px_rs, g).wait_recv()
        to_partner(g_rows, pg_ss, pg_rs, g).wait_recv()
        acts_copy(g).wait_recv()

    total_rows = 2 * groups * rows
    for i in range(3):
        acts_t[pl.ds(i * hidden, hidden), :] = (
            acts[:, :, :, pl.ds(i * hidden, hidden)].reshape(total_rows, hidden).T
        )
    share = 1.0 / batches

    @pl.loop(0, width // 256)
    def _(t):
        columns = pl.ds(pl.multiple_of(t * 256, 128), 256)
        rows_in = x_rows[:, :, :, :, columns].reshape(total_rows, 256)
        rows_grad = g_rows[:, :, :, :, columns].reshape(total_rows, 256)
        for i, (result, side) in enumerate(
            ((dwg_ref, rows_in), (dwu_ref, rows_in), (dwd_ref, rows_grad))
        ):
            grad = jnp.dot(
                acts_t[pl.ds(i * hidden, hidden), :], side, preferred_element_type=F32
            )
            result[:, columns] = (grad * share).astype(BF16)

    @pl.loop(0, groups)
    def _(g):
        wait_sent(x_send, x_rows.at[0], x_ss, x_rs, g)
        wait_sent(g_send, g_rows.at[0], g_ss, g_rs, g)
        wait_sent(r_send, r_recv, r_ss, r_rs, g)
        to_partner(x_rows, px_ss, px_rs, g).wait_send()
        to_partner(g_rows, pg_ss, pg_rs, g).wait_send()
        acts_copy(g).wait_send()

        @pl.when(section > 0)
        def _():
            hop_copy(g).wait_send()

        if not gathered:
            @pl.when(jnp.logical_not(last))
            def _():
                top_copy(g).wait_send()

    for copy in weight_copies:
        copy.wait_send()


def on_device(group_rows, x_saved, routes, gates, cotangent, w_gate, w_up, w_down):
    sections = lax.axis_size("section")
    experts = lax.axis_size("expert") // SPLIT
    batches, tokens, width = x_saved.shape[1:]
    top = routes.shape[3]
    hidden = w_gate.shape[1]
    capacity = max(2, 3 * tokens * top // (2 * experts))
    per = 1
    while per * capacity < group_rows and batches % (2 * per) == 0:
        per *= 2
    groups = batches // per
    blk = -(-per * capacity // 16) * 16
    rows = experts * blk
    pair = 2 if groups % 2 == 0 else 1
    tile = 512 if width % 512 == 0 else 128

    flat = routes[0].reshape(batches, tokens * top)
    hot = (flat[:, :, None] == jnp.arange(experts, dtype=jnp.int32)).astype(jnp.int32)
    earlier = jnp.cumsum(hot, axis=1) - hot
    within = jnp.sum(earlier * hot, axis=2)
    batch_in = jnp.arange(batches, dtype=jnp.int32)[:, None] % per
    target = (flat * blk + batch_in * capacity + within).reshape(groups, per, tokens, top)
    target = jnp.transpose(target, (0, 3, 1, 2)).reshape(groups, top, per * tokens)
    spots = jnp.arange(rows, dtype=jnp.int32)
    place = (spots[None, :, None] == target.reshape(groups, 1, -1)).astype(BF16)
    place_x = jnp.any(spots[None, :, None, None] == target[:, None], axis=2).astype(BF16)
    place_t = jnp.any(target[:, :, :, None] == spots, axis=1).astype(BF16)
    scales = jnp.transpose(
        gates[0].reshape(groups, per * tokens, top), (0, 2, 1)
    )[..., None]
    x_groups = x_saved[0].reshape(groups, per * tokens, width)
    if cotangent.shape[2] % 128:
        cotangent = lax.all_gather(cotangent, "section", axis=2, tiled=True)
    cot_groups = cotangent.reshape(groups, per * tokens, cotangent.shape[2])

    vmem = pl.BlockSpec(memory_space=pltpu.VMEM)
    slots = (groups, experts, blk, width)
    dma = pltpu.SemaphoreType.DMA
    grad_w = jax.ShapeDtypeStruct((hidden, width), BF16)
    results = pl.pallas_call(
        functools.partial(relay_kernel, sections, experts, batches, groups, pair, blk, tile),
        out_shape=(
            jax.ShapeDtypeStruct((groups, per * tokens, width), BF16), grad_w, grad_w, grad_w,
        ),
        in_specs=[vmem] * 6 + [pl.BlockSpec(memory_space=pl.ANY)] * 3,
        out_specs=(vmem,) * 4,
        scratch_shapes=[
            pltpu.VMEM((groups, per * tokens, width), BF16),
            pltpu.VMEM(slots, BF16),
            pltpu.VMEM((2,) + slots, BF16),
            pltpu.VMEM(slots, BF16),
            pltpu.VMEM((2,) + slots, BF16),
            pltpu.VMEM(slots, BF16),
            pltpu.VMEM(slots, BF16),
            pltpu.VMEM((4 * hidden, width), BF16),
            pltpu.VMEM((2 * hidden, width), BF16),
            pltpu.VMEM((2, groups, rows, 3 * hidden), BF16),
            pltpu.VMEM((groups, rows, 3 * hidden), BF16),
            pltpu.VMEM((3 * hidden, 2 * groups * rows), BF16),
            pltpu.VMEM((groups, rows, 2 * hidden), F32),
            pltpu.VMEM((groups, rows, 2 * hidden), F32),
        ]
        + [dma((groups, experts))] * 6
        + [dma((groups,)), dma((groups,)), dma((groups,)), dma((groups, sections))]
        + [dma((3,))] * 3
        + [dma((groups,))] * 6,
        compiler_params=pltpu.CompilerParams(
            collective_id=0, has_side_effects=True, vmem_limit_bytes=60 * 2**20
        ),
    )(
        x_groups, cot_groups, scales, place, place_x, place_t, w_gate[0], w_up[0], w_down[0]
    )
    grad_inputs = results[0].reshape(1, batches, tokens, width)
    return (grad_inputs, results[1][None], results[2][None], results[3][None])


def solution(mesh):
    rows = P("section", None, "expert", None)
    halves = P("section", "expert", None)
    return jax.shard_map(
        functools.partial(on_device, 12), mesh=mesh,
        in_specs=(rows, rows, rows, P(None, "expert", "section"), halves, halves, halves),
        out_specs=(rows, halves, halves, halves),
        check_vma=False,
    )
```

```python
import functools

import jax
import jax.numpy as jnp
import numpy as np
from jax import lax
from jax.experimental import pallas as pl
from jax.experimental.pallas import tpu as pltpu
from jax.sharding import PartitionSpec as P

SPLIT = 2
MESH = pl.DeviceIdType.MESH
COLS = (((1,), (1,)), ((), ()))
F32 = jnp.float32
BF16 = jnp.bfloat16


def relay_kernel(
    sections, experts, batches, groups, pair, fold,
    x_ref, cot_ref, gates_ref, keys_ref, spots_ref, unpack_ref, pack_ref, wg_ref, wu_ref, wd_ref,
    out_ref, dwg_ref, dwu_ref, dwd_ref,
    up_buf, x_send, x_wire, x_rows, g_send, g_wire, g_rows, r_send, r_recv, w_gu, w_d, acts, acts_send, acts_t,
    slope_buf, swish_buf,
    x_ss, x_rs, g_ss, g_rs, r_ss, r_rs, hop_ss, hop_rs, top_ss, top_rs, w_ss, w_rs, w_ls,
    px_ss, px_rs, pg_ss, pg_rs, pa_ss, pa_rs,
):
    section = lax.axis_index("section")
    place_in = lax.axis_index("expert")
    chip = place_in // SPLIT
    core = place_in % SPLIT
    other = chip * SPLIT + (1 - core)
    last = section == sections - 1
    rows = x_rows.shape[2]
    width = x_ref.shape[2]
    chunk = width // fold
    wire = x_send.shape[1:]
    hidden = wg_ref.shape[0]
    piece = cot_ref.shape[2]
    gathered = piece == width

    def remote(src, dst, ss, rs, sec, exp):
        return pltpu.make_async_remote_copy(
            src_ref=src, dst_ref=dst, send_sem=ss, recv_sem=rs,
            device_id=(sec, exp), device_id_type=MESH,
        )

    def peer(step):
        return lax.rem(chip + step, experts)

    own_w = (wg_ref, wu_ref, wd_ref)
    own_at = [w_gu.at[pl.ds(0, hidden)], w_gu.at[pl.ds(hidden, hidden)], w_d.at[pl.ds(0, hidden)]]
    other_at = [
        w_gu.at[pl.ds(2 * hidden, hidden)], w_gu.at[pl.ds(3 * hidden, hidden)],
        w_d.at[pl.ds(hidden, hidden)],
    ]
    local_copies = [
        pltpu.make_async_copy(own_w[i], own_at[i], w_ls.at[i]) for i in range(3)
    ]
    for copy in local_copies:
        copy.start()

    barrier = pltpu.get_barrier_semaphore()
    for step in range(1, experts):
        pl.semaphore_signal(
            barrier, inc=1, device_id=(section, peer(step) * SPLIT + core), device_id_type=MESH
        )
    pl.semaphore_signal(barrier, inc=1, device_id=(section, other), device_id_type=MESH)
    for step in range(1, sections):
        pl.semaphore_signal(
            barrier, inc=1, device_id=(lax.rem(section + step, sections), place_in),
            device_id_type=MESH,
        )
    pl.semaphore_wait(barrier, experts - 1 + 1 + sections - 1)

    def exchange(send, recv, ss, rs, g, step):
        to = peer(step)
        return remote(
            send.at[g, to], recv.at[g, chip], ss.at[g, to], rs.at[g, chip],
            section, to * SPLIT + core,
        )

    def arrival(send, recv, ss, rs, g, step):
        source = peer(step)
        return remote(
            send.at[g, source], recv.at[g, source], ss.at[g, source], rs.at[g, source],
            section, source * SPLIT + core,
        )

    def send_all(send, recv, ss, rs, g):
        for step in range(1, experts):
            exchange(send, recv, ss, rs, g, step).start()

    def wait_all(send, recv, ss, rs, g):
        for step in range(1, experts):
            arrival(send, recv, ss, rs, g, step).wait_recv()

    def wait_sent(send, recv, ss, rs, g):
        for step in range(1, experts):
            exchange(send, recv, ss, rs, g, step).wait_send()

    def top_copy(g):
        return remote(
            cot_ref.at[g], up_buf.at[g, :, pl.ds(pl.multiple_of(section * piece, 128), piece)],
            top_ss.at[g], top_rs.at[g, section], sections - 1, place_in,
        )

    def hop_copy(g):
        return remote(
            out_ref.at[g], up_buf.at[g], hop_ss.at[g], hop_rs.at[g],
            jnp.maximum(section - 1, 0), place_in,
        )

    def one_hot(g, k):
        return jnp.where(spots_ref[...] == keys_ref[g, k], 1.0, 0.0).astype(BF16)

    def both_hot(g):
        hot = one_hot(g, 0)
        for k in range(1, keys_ref.shape[1]):
            hot = hot + one_hot(g, k)
        return hot

    def stacked(value):
        return jnp.concatenate(
            [value[:, c * chunk : (c + 1) * chunk] for c in range(fold)], axis=0
        )

    def side_by_side(value, count):
        return jnp.concatenate(
            [value[c * count : (c + 1) * count] for c in range(fold)], axis=1
        )

    def unpacked(buf, g):
        return side_by_side(
            jnp.dot(
                unpack_ref[...], buf[g].reshape(fold * rows, chunk), preferred_element_type=F32
            ).astype(BF16),
            rows,
        )

    def to_partner(buf, ss, rs, g):
        return remote(buf.at[0, g], buf.at[1, g], ss.at[g], rs.at[g], section, other)

    def acts_copy(g):
        return remote(
            acts_send.at[g], acts.at[1, g], pa_ss.at[g], pa_rs.at[g], section, other
        )

    weight_copies = [
        remote(own_w[i], other_at[i], w_ss.at[i], w_rs.at[i], section, other) for i in range(3)
    ]

    ahead = jnp.where(last, min(pair, groups), groups)
    for copy in weight_copies:
        copy.start()

    @pl.loop(0, groups)
    def _(g):
        if not gathered:
            @pl.when(jnp.logical_not(last))
            def _():
                top_copy(g).start()

        placed = jnp.dot(both_hot(g), stacked(x_ref[g]), preferred_element_type=F32)
        x_send[g] = placed.astype(BF16).reshape(wire)

        @pl.when(g < ahead)
        def _():
            send_all(x_send, x_wire, x_ss, x_rs, g)

        x_wire[g, chip] = x_send[g, chip]

    def rows_arrived(g):
        wait_all(x_send, x_wire, x_ss, x_rs, g)
        x_rows[0, g] = unpacked(x_wire, g)
        to_partner(x_rows, px_ss, px_rs, g).start()

    def forward(p):
        first = p * pair
        for i in range(pair):
            rows_arrived(first + i)
        members = pl.ds(first, pair)
        rows_in = x_rows[0, members].reshape(pair * rows, width)
        for half in range(2):
            both = lax.dot_general(
                rows_in, w_gu[pl.ds(half * 2 * hidden, 2 * hidden), :], COLS,
                preferred_element_type=F32,
            )
            pre_gate, pre_up = both[:, :hidden], both[:, hidden:]
            sigmoid = jax.nn.sigmoid(pre_gate)
            swished = pre_gate * sigmoid
            slope = pre_up * (sigmoid * (1.0 + pre_gate * (1.0 - sigmoid)))
            act = (swished * pre_up).astype(BF16)
            columns = pl.ds(half * hidden, hidden)
            swish_buf[members, :, columns] = swished.reshape(pair, rows, hidden)
            slope_buf[members, :, columns] = slope.reshape(pair, rows, hidden)
            third = pl.ds(2 * hidden, hidden)
            if half == 0:
                acts[0, members, :, third] = act.reshape(pair, rows, hidden)
            else:
                acts_send[members, :, third] = act.reshape(pair, rows, hidden)

    def dispatch(g):
        @pl.when(last)
        def _():
            if gathered:
                up_buf[g] = cot_ref[g]
            else:
                for z in range(sections - 1):
                    remote(
                        cot_ref.at[g], up_buf.at[g, :, pl.ds(z * piece, piece)],
                        top_ss.at[g], top_rs.at[g, z], section, place_in,
                    ).wait_recv()
                up_buf[g, :, pl.ds((sections - 1) * piece, piece)] = cot_ref[g]

        @pl.when(jnp.logical_not(last))
        def _():
            hop_copy(g).wait_recv()

        upstream = up_buf[g].astype(F32)
        placed = jnp.zeros((fold * rows, chunk), F32)
        for k in range(gates_ref.shape[1]):
            scaled = (upstream * gates_ref[g, k]).astype(BF16)
            placed += jnp.dot(one_hot(g, k), stacked(scaled), preferred_element_type=F32)
        g_send[g] = placed.astype(BF16).reshape(wire)
        send_all(g_send, g_wire, g_ss, g_rs, g)
        g_wire[g, chip] = g_send[g, chip]

    def backward(g):
        wait_all(g_send, g_wire, g_ss, g_rs, g)
        rows_grad = unpacked(g_wire, g)
        g_rows[0, g] = rows_grad
        d_hidden = lax.dot_general(rows_grad, w_d[...], COLS, preferred_element_type=F32)
        d_gate = (d_hidden * slope_buf[g]).astype(BF16)
        d_up = (d_hidden * swish_buf[g]).astype(BF16)
        slopes = jnp.concatenate(
            [d_gate[:, :hidden], d_up[:, :hidden], d_gate[:, hidden:], d_up[:, hidden:]], axis=1
        )
        acts[0, g, :, pl.ds(0, 2 * hidden)] = slopes[:, : 2 * hidden]
        acts_send[g, :, pl.ds(0, 2 * hidden)] = slopes[:, 2 * hidden :]

        half = width // 2
        total = jnp.concatenate(
            [
                jnp.dot(
                    slopes, w_gu[:, pl.ds(i * half, half)], preferred_element_type=F32
                ).astype(BF16)
                for i in range(2)
            ],
            axis=1,
        )
        packed = jnp.dot(pack_ref[...], stacked(total), preferred_element_type=F32)
        r_send[g] = packed.astype(BF16).reshape(wire)
        send_all(r_send, r_recv, r_ss, r_rs, g)
        r_recv[g, chip] = r_send[g, chip]
        to_partner(g_rows, pg_ss, pg_rs, g).start()
        acts_copy(g).start()

    def combine(g):
        wait_all(r_send, r_recv, r_ss, r_rs, g)
        picked = lax.dot_general(
            both_hot(g), r_recv[g].reshape(fold * rows, chunk), (((0,), (0,)), ((), ())),
            preferred_element_type=F32,
        )
        back = side_by_side(picked, x_ref.shape[1])
        out_ref[g] = (up_buf[g].astype(F32) + back).astype(BF16)

        @pl.when(section > 0)
        def _():
            hop_copy(g).start()

    for i in range(2):
        local_copies[i].wait()
        weight_copies[i].wait_recv()

    @pl.loop(0, jnp.where(last, 0, groups // pair))
    def _(p):
        forward(p)

    local_copies[2].wait()
    weight_copies[2].wait_recv()

    @pl.loop(0, groups + 1)
    def _(g):
        @pl.when(g < groups)
        def _():
            dispatch(g)

        @pl.when(jnp.logical_and(last, g + pair < groups))
        def _():
            send_all(x_send, x_wire, x_ss, x_rs, g + pair)

        @pl.when(jnp.logical_and(last, jnp.logical_and(g < groups, lax.rem(g, pair) == 0)))
        def _():
            forward(g // pair)

        @pl.when(g > 0)
        def _():
            combine(g - 1)

        @pl.when(g < groups)
        def _():
            backward(g)

    @pl.loop(0, groups)
    def _(g):
        to_partner(x_rows, px_ss, px_rs, g).wait_recv()
        to_partner(g_rows, pg_ss, pg_rs, g).wait_recv()
        acts_copy(g).wait_recv()

    total_rows = 2 * groups * rows
    for i in range(3):
        acts_t[pl.ds(i * hidden, hidden), :] = (
            acts[:, :, :, pl.ds(i * hidden, hidden)].reshape(total_rows, hidden).T
        )
    share = 1.0 / batches

    @pl.loop(0, width // 256)
    def _(t):
        columns = pl.ds(pl.multiple_of(t * 256, 128), 256)
        rows_in = x_rows[:, :, :, columns].reshape(total_rows, 256)
        rows_grad = g_rows[:, :, :, columns].reshape(total_rows, 256)
        for i, (result, side) in enumerate(
            ((dwg_ref, rows_in), (dwu_ref, rows_in), (dwd_ref, rows_grad))
        ):
            grad = jnp.dot(
                acts_t[pl.ds(i * hidden, hidden), :], side, preferred_element_type=F32
            )
            result[:, columns] = (grad * share).astype(BF16)

    @pl.loop(0, groups)
    def _(g):
        wait_sent(x_send, x_wire, x_ss, x_rs, g)
        wait_sent(g_send, g_wire, g_ss, g_rs, g)
        wait_sent(r_send, r_recv, r_ss, r_rs, g)
        to_partner(x_rows, px_ss, px_rs, g).wait_send()
        to_partner(g_rows, pg_ss, pg_rs, g).wait_send()
        acts_copy(g).wait_send()

        @pl.when(section > 0)
        def _():
            hop_copy(g).wait_send()

        if not gathered:
            @pl.when(jnp.logical_not(last))
            def _():
                top_copy(g).wait_send()

    for copy in weight_copies:
        copy.wait_send()


def on_device(group_rows, x_saved, routes, gates, cotangent, w_gate, w_up, w_down):
    sections = lax.axis_size("section")
    experts = lax.axis_size("expert") // SPLIT
    batches, tokens, width = x_saved.shape[1:]
    top = routes.shape[3]
    hidden = w_gate.shape[1]
    capacity = max(2, 3 * tokens * top // (2 * experts))
    per = 1
    while per * capacity < group_rows and batches % (2 * per) == 0:
        per *= 2
    groups = batches // per
    block = per * capacity
    fold = 0
    for parts in (4, 2, 1):
        if block * parts % 16 == 0 and experts * block % 16 == 0 and width % (128 * parts) == 0:
            fold = parts
    if fold == 0:
        fold, block = 1, -(-block // 16) * 16
    rows = experts * block
    pair = 2 if groups % 2 == 0 else 1

    flat = routes[0].reshape(batches, tokens * top)
    hot = (flat[:, :, None] == jnp.arange(experts, dtype=jnp.int32)).astype(jnp.int32)
    earlier = jnp.cumsum(hot, axis=1) - hot
    within = jnp.sum(earlier * hot, axis=2)
    batch_in = jnp.arange(batches, dtype=jnp.int32)[:, None] % per
    target = (flat * block + batch_in * capacity + within).reshape(groups, per, tokens, top)
    target = jnp.transpose(target, (0, 3, 1, 2)).reshape(groups, top, 1, per * tokens)
    chunks = jnp.arange(fold, dtype=jnp.int32)[:, None] * rows
    keys = (target + chunks).reshape(groups, top, 1, fold * per * tokens)
    on_wire = np.transpose(
        np.arange(fold * rows, dtype=np.int32).reshape(fold, experts, block), (1, 0, 2)
    ).reshape(-1)
    spots = np.repeat(on_wire[:, None], fold * per * tokens, axis=1)
    pack = (on_wire[:, None] == np.arange(fold * rows)[None, :]).astype(np.float32)
    scales = jnp.transpose(
        gates[0].reshape(groups, per * tokens, top), (0, 2, 1)
    )[..., None]
    x_groups = x_saved[0].reshape(groups, per * tokens, width)
    if cotangent.shape[2] % 128:
        cotangent = lax.all_gather(cotangent, "section", axis=2, tiled=True)
    cot_groups = cotangent.reshape(groups, per * tokens, cotangent.shape[2])

    vmem = pl.BlockSpec(memory_space=pltpu.VMEM)
    slots = (groups, experts, fold * block, width // fold)
    whole = (2, groups, rows, width)
    dma = pltpu.SemaphoreType.DMA
    grad_w = jax.ShapeDtypeStruct((hidden, width), BF16)
    results = pl.pallas_call(
        functools.partial(relay_kernel, sections, experts, batches, groups, pair, fold),
        out_shape=(
            jax.ShapeDtypeStruct((groups, per * tokens, width), BF16), grad_w, grad_w, grad_w,
        ),
        in_specs=[vmem] * 7 + [pl.BlockSpec(memory_space=pl.ANY)] * 3,
        out_specs=(vmem,) * 4,
        scratch_shapes=[
            pltpu.VMEM((groups, per * tokens, width), BF16),
            pltpu.VMEM(slots, BF16),
            pltpu.VMEM(slots, BF16),
            pltpu.VMEM(whole, BF16),
            pltpu.VMEM(slots, BF16),
            pltpu.VMEM(slots, BF16),
            pltpu.VMEM(whole, BF16),
            pltpu.VMEM(slots, BF16),
            pltpu.VMEM(slots, BF16),
            pltpu.VMEM((4 * hidden, width), BF16),
            pltpu.VMEM((2 * hidden, width), BF16),
            pltpu.VMEM((2, groups, rows, 3 * hidden), BF16),
            pltpu.VMEM((groups, rows, 3 * hidden), BF16),
            pltpu.VMEM((3 * hidden, 2 * groups * rows), BF16),
            pltpu.VMEM((groups, rows, 2 * hidden), F32),
            pltpu.VMEM((groups, rows, 2 * hidden), F32),
        ]
        + [dma((groups, experts))] * 6
        + [dma((groups,)), dma((groups,)), dma((groups,)), dma((groups, sections))]
        + [dma((3,))] * 3
        + [dma((groups,))] * 6,
        compiler_params=pltpu.CompilerParams(
            collective_id=0, has_side_effects=True, vmem_limit_bytes=60 * 2**20
        ),
    )(
        x_groups, cot_groups, scales, keys, jnp.asarray(spots),
        jnp.asarray(pack.T, BF16), jnp.asarray(pack, BF16), w_gate[0], w_up[0], w_down[0]
    )
    grad_inputs = results[0].reshape(1, batches, tokens, width)
    return (grad_inputs, results[1][None], results[2][None], results[3][None])


def solution(mesh):
    rows = P("section", None, "expert", None)
    halves = P("section", "expert", None)
    return jax.shard_map(
        functools.partial(on_device, 12), mesh=mesh,
        in_specs=(rows, rows, rows, P(None, "expert", "section"), halves, halves, halves),
        out_specs=(rows, halves, halves, halves),
        check_vma=False,
    )
```

```python
import functools

import jax
import jax.numpy as jnp
import numpy as np
from jax import lax
from jax.experimental import pallas as pl
from jax.experimental.pallas import tpu as pltpu
from jax.sharding import PartitionSpec as P

SPLIT = 2
MESH = pl.DeviceIdType.MESH
COLS = (((1,), (1,)), ((), ()))
F32 = jnp.float32
BF16 = jnp.bfloat16


def relay_kernel(
    sections, experts, batches, groups, pair, fold,
    x_ref, cot_ref, gates_ref, keys_ref, spots_ref, unpack_ref, pack_ref, wg_ref, wu_ref, wd_ref,
    out_ref, dwg_ref, dwu_ref, dwd_ref,
    up_buf, x_send, x_wire, x_rows, g_send, g_wire, g_rows, r_send, r_recv, w_gu, w_d, acts, acts_send, acts_t,
    slope_buf, swish_buf,
    x_ss, x_rs, g_ss, g_rs, r_ss, r_rs, hop_ss, hop_rs, top_ss, top_rs, w_ss, w_rs, w_ls,
    px_ss, px_rs, pg_ss, pg_rs, pa_ss, pa_rs,
):
    section = lax.axis_index("section")
    place_in = lax.axis_index("expert")
    chip = place_in // SPLIT
    core = place_in % SPLIT
    other = chip * SPLIT + (1 - core)
    last = section == sections - 1
    rows = x_rows.shape[2]
    width = x_ref.shape[2]
    chunk = width // fold
    wire = x_send.shape[1:]
    hidden = wg_ref.shape[0]
    piece = cot_ref.shape[2]
    gathered = piece == width

    def remote(src, dst, ss, rs, sec, exp):
        return pltpu.make_async_remote_copy(
            src_ref=src, dst_ref=dst, send_sem=ss, recv_sem=rs,
            device_id=(sec, exp), device_id_type=MESH,
        )

    def peer(step):
        return lax.rem(chip + step, experts)

    own_w = (wg_ref, wu_ref, wd_ref)
    own_at = [w_gu.at[pl.ds(0, hidden)], w_gu.at[pl.ds(hidden, hidden)], w_d.at[pl.ds(0, hidden)]]
    other_at = [
        w_gu.at[pl.ds(2 * hidden, hidden)], w_gu.at[pl.ds(3 * hidden, hidden)],
        w_d.at[pl.ds(hidden, hidden)],
    ]
    local_copies = [
        pltpu.make_async_copy(own_w[i], own_at[i], w_ls.at[i]) for i in range(3)
    ]
    for copy in local_copies:
        copy.start()

    barrier = pltpu.get_barrier_semaphore()
    for step in range(1, experts):
        pl.semaphore_signal(
            barrier, inc=1, device_id=(section, peer(step) * SPLIT + core), device_id_type=MESH
        )
    pl.semaphore_signal(barrier, inc=1, device_id=(section, other), device_id_type=MESH)
    for step in range(1, sections):
        pl.semaphore_signal(
            barrier, inc=1, device_id=(lax.rem(section + step, sections), place_in),
            device_id_type=MESH,
        )
    pl.semaphore_wait(barrier, experts - 1 + 1 + sections - 1)

    def exchange(send, recv, ss, rs, g, step):
        to = peer(step)
        return remote(
            send.at[g, to], recv.at[g, chip], ss.at[g, to], rs.at[g, chip],
            section, to * SPLIT + core,
        )

    def arrival(send, recv, ss, rs, g, step):
        source = peer(step)
        return remote(
            send.at[g, source], recv.at[g, source], ss.at[g, source], rs.at[g, source],
            section, source * SPLIT + core,
        )

    def send_all(send, recv, ss, rs, g):
        for step in range(1, experts):
            exchange(send, recv, ss, rs, g, step).start()

    def wait_all(send, recv, ss, rs, g):
        for step in range(1, experts):
            arrival(send, recv, ss, rs, g, step).wait_recv()

    def wait_sent(send, recv, ss, rs, g):
        for step in range(1, experts):
            exchange(send, recv, ss, rs, g, step).wait_send()

    def top_copy(g):
        return remote(
            cot_ref.at[g], up_buf.at[g, :, pl.ds(pl.multiple_of(section * piece, 128), piece)],
            top_ss.at[g], top_rs.at[g, section], sections - 1, place_in,
        )

    def hop_copy(g):
        return remote(
            out_ref.at[g], up_buf.at[g], hop_ss.at[g], hop_rs.at[g],
            jnp.maximum(section - 1, 0), place_in,
        )

    def one_hot(g, k):
        return jnp.where(spots_ref[...] == keys_ref[g, k], 1.0, 0.0).astype(BF16)

    def both_hot(g):
        hot = one_hot(g, 0)
        for k in range(1, keys_ref.shape[1]):
            hot = hot + one_hot(g, k)
        return hot

    def stacked(value):
        return jnp.concatenate(
            [value[:, c * chunk : (c + 1) * chunk] for c in range(fold)], axis=0
        )

    def side_by_side(value, count):
        return jnp.concatenate(
            [value[c * count : (c + 1) * count] for c in range(fold)], axis=1
        )

    def unpacked(buf, g):
        return side_by_side(
            jnp.dot(
                unpack_ref[...], buf[g].reshape(fold * rows, chunk), preferred_element_type=F32
            ).astype(BF16),
            rows,
        )

    def to_partner(buf, ss, rs, g):
        return remote(buf.at[0, g], buf.at[1, g], ss.at[g], rs.at[g], section, other)

    def acts_copy(g):
        return remote(
            acts_send.at[g], acts.at[1, g], pa_ss.at[g], pa_rs.at[g], section, other
        )

    weight_copies = [
        remote(own_w[i], other_at[i], w_ss.at[i], w_rs.at[i], section, other) for i in range(3)
    ]

    ahead = jnp.where(last, min(pair, groups), groups)
    for copy in weight_copies:
        copy.start()

    def place_inputs(g):
        placed = jnp.dot(both_hot(g), stacked(x_ref[g]), preferred_element_type=F32)
        x_send[g] = placed.astype(BF16).reshape(wire)
        x_wire[g, chip] = x_send[g, chip]

    if not gathered:
        @pl.when(jnp.logical_not(last))
        def _():
            @pl.loop(0, groups)
            def _(g):
                top_copy(g).start()

    @pl.loop(0, ahead)
    def _(g):
        place_inputs(g)
        send_all(x_send, x_wire, x_ss, x_rs, g)

    def rows_arrived(g):
        wait_all(x_send, x_wire, x_ss, x_rs, g)
        x_rows[0, g] = unpacked(x_wire, g)
        to_partner(x_rows, px_ss, px_rs, g).start()

    def forward(p):
        first = p * pair
        for i in range(pair):
            rows_arrived(first + i)
        members = pl.ds(first, pair)
        rows_in = x_rows[0, members].reshape(pair * rows, width)
        for half in range(2):
            both = lax.dot_general(
                rows_in, w_gu[pl.ds(half * 2 * hidden, 2 * hidden), :], COLS,
                preferred_element_type=F32,
            )
            pre_gate, pre_up = both[:, :hidden], both[:, hidden:]
            sigmoid = jax.nn.sigmoid(pre_gate)
            swished = pre_gate * sigmoid
            slope = pre_up * (sigmoid * (1.0 + pre_gate * (1.0 - sigmoid)))
            act = (swished * pre_up).astype(BF16)
            columns = pl.ds(half * hidden, hidden)
            swish_buf[members, :, columns] = swished.reshape(pair, rows, hidden)
            slope_buf[members, :, columns] = slope.reshape(pair, rows, hidden)
            third = pl.ds(2 * hidden, hidden)
            if half == 0:
                acts[0, members, :, third] = act.reshape(pair, rows, hidden)
            else:
                acts_send[members, :, third] = act.reshape(pair, rows, hidden)

    def dispatch(g):
        @pl.when(last)
        def _():
            if gathered:
                up_buf[g] = cot_ref[g]
            else:
                for z in range(sections - 1):
                    remote(
                        cot_ref.at[g], up_buf.at[g, :, pl.ds(z * piece, piece)],
                        top_ss.at[g], top_rs.at[g, z], section, place_in,
                    ).wait_recv()
                up_buf[g, :, pl.ds((sections - 1) * piece, piece)] = cot_ref[g]

        @pl.when(jnp.logical_not(last))
        def _():
            hop_copy(g).wait_recv()

        upstream = up_buf[g].astype(F32)
        placed = jnp.zeros((fold * rows, chunk), F32)
        for k in range(gates_ref.shape[1]):
            scaled = (upstream * gates_ref[g, k]).astype(BF16)
            placed += jnp.dot(one_hot(g, k), stacked(scaled), preferred_element_type=F32)
        g_send[g] = placed.astype(BF16).reshape(wire)
        send_all(g_send, g_wire, g_ss, g_rs, g)
        g_wire[g, chip] = g_send[g, chip]

    def backward(g):
        wait_all(g_send, g_wire, g_ss, g_rs, g)

        @pl.when(jnp.logical_and(last, g + pair < groups))
        def _():
            send_all(x_send, x_wire, x_ss, x_rs, g + pair)

        rows_grad = unpacked(g_wire, g)
        g_rows[0, g] = rows_grad
        d_hidden = lax.dot_general(rows_grad, w_d[...], COLS, preferred_element_type=F32)
        d_gate = (d_hidden * slope_buf[g]).astype(BF16)
        d_up = (d_hidden * swish_buf[g]).astype(BF16)
        slopes = jnp.concatenate(
            [d_gate[:, :hidden], d_up[:, :hidden], d_gate[:, hidden:], d_up[:, hidden:]], axis=1
        )
        acts[0, g, :, pl.ds(0, 2 * hidden)] = slopes[:, : 2 * hidden]
        acts_send[g, :, pl.ds(0, 2 * hidden)] = slopes[:, 2 * hidden :]

        half = width // 2
        total = jnp.concatenate(
            [
                jnp.dot(
                    slopes, w_gu[:, pl.ds(i * half, half)], preferred_element_type=F32
                ).astype(BF16)
                for i in range(2)
            ],
            axis=1,
        )
        packed = jnp.dot(pack_ref[...], stacked(total), preferred_element_type=F32)
        r_send[g] = packed.astype(BF16).reshape(wire)
        send_all(r_send, r_recv, r_ss, r_rs, g)
        r_recv[g, chip] = r_send[g, chip]
        to_partner(g_rows, pg_ss, pg_rs, g).start()
        acts_copy(g).start()

    def combine(g):
        wait_all(r_send, r_recv, r_ss, r_rs, g)
        picked = lax.dot_general(
            both_hot(g), r_recv[g].reshape(fold * rows, chunk), (((0,), (0,)), ((), ())),
            preferred_element_type=F32,
        )
        back = side_by_side(picked, x_ref.shape[1])
        out_ref[g] = (up_buf[g].astype(F32) + back).astype(BF16)

        @pl.when(section > 0)
        def _():
            hop_copy(g).start()

    def wait_weights(first, end):
        for i in range(first, end):
            local_copies[i].wait()
            weight_copies[i].wait_recv()

    pairs = groups // pair
    upfront = jnp.minimum(2 * (sections - 1 - section), pairs)

    @pl.when(jnp.logical_not(last))
    def _():
        wait_weights(0, 2)

        @pl.loop(0, upfront)
        def _(p):
            forward(p)

    @pl.loop(0, groups + 1)
    def _(g):
        @pl.when(g < groups)
        def _():
            dispatch(g)

        @pl.when(jnp.logical_and(last, g + pair < groups))
        def _():
            place_inputs(g + pair)

        @pl.when(jnp.logical_and(last, g == 0))
        def _():
            wait_weights(0, 2)

        @pl.when(jnp.logical_and(g // pair + upfront < pairs, lax.rem(g, pair) == 0))
        def _():
            forward(g // pair + upfront)

        @pl.when(g == 0)
        def _():
            wait_weights(2, 3)

        @pl.when(g > 0)
        def _():
            combine(g - 1)

        @pl.when(g < groups)
        def _():
            backward(g)

    @pl.loop(0, groups)
    def _(g):
        to_partner(x_rows, px_ss, px_rs, g).wait_recv()
        to_partner(g_rows, pg_ss, pg_rs, g).wait_recv()
        acts_copy(g).wait_recv()

    total_rows = 2 * groups * rows
    for i in range(3):
        acts_t[pl.ds(i * hidden, hidden), :] = (
            acts[:, :, :, pl.ds(i * hidden, hidden)].reshape(total_rows, hidden).T
        )
    share = 1.0 / batches

    @pl.loop(0, width // 256)
    def _(t):
        columns = pl.ds(pl.multiple_of(t * 256, 128), 256)
        rows_in = x_rows[:, :, :, columns].reshape(total_rows, 256)
        rows_grad = g_rows[:, :, :, columns].reshape(total_rows, 256)
        for i, (result, side) in enumerate(
            ((dwg_ref, rows_in), (dwu_ref, rows_in), (dwd_ref, rows_grad))
        ):
            grad = jnp.dot(
                acts_t[pl.ds(i * hidden, hidden), :], side, preferred_element_type=F32
            )
            result[:, columns] = (grad * share).astype(BF16)

    @pl.loop(0, groups)
    def _(g):
        wait_sent(x_send, x_wire, x_ss, x_rs, g)
        wait_sent(g_send, g_wire, g_ss, g_rs, g)
        wait_sent(r_send, r_recv, r_ss, r_rs, g)
        to_partner(x_rows, px_ss, px_rs, g).wait_send()
        to_partner(g_rows, pg_ss, pg_rs, g).wait_send()
        acts_copy(g).wait_send()

        @pl.when(section > 0)
        def _():
            hop_copy(g).wait_send()

        if not gathered:
            @pl.when(jnp.logical_not(last))
            def _():
                top_copy(g).wait_send()

    for copy in weight_copies:
        copy.wait_send()


def on_device(group_rows, x_saved, routes, gates, cotangent, w_gate, w_up, w_down):
    sections = lax.axis_size("section")
    experts = lax.axis_size("expert") // SPLIT
    batches, tokens, width = x_saved.shape[1:]
    top = routes.shape[3]
    hidden = w_gate.shape[1]
    capacity = max(2, 3 * tokens * top // (2 * experts))
    per = 1
    while per * capacity < group_rows and batches % (2 * per) == 0:
        per *= 2
    groups = batches // per
    block = per * capacity
    fold = 0
    for parts in (4, 2, 1):
        if block * parts % 16 == 0 and experts * block % 16 == 0 and width % (128 * parts) == 0:
            fold = parts
    if fold == 0:
        fold, block = 1, -(-block // 16) * 16
    rows = experts * block
    pair = 2 if groups % 2 == 0 else 1

    flat = routes[0].reshape(batches, tokens * top)
    hot = (flat[:, :, None] == jnp.arange(experts, dtype=jnp.int32)).astype(jnp.int32)
    earlier = jnp.cumsum(hot, axis=1) - hot
    within = jnp.sum(earlier * hot, axis=2)
    batch_in = jnp.arange(batches, dtype=jnp.int32)[:, None] % per
    target = (flat * block + batch_in * capacity + within).reshape(groups, per, tokens, top)
    target = jnp.transpose(target, (0, 3, 1, 2)).reshape(groups, top, 1, per * tokens)
    chunks = jnp.arange(fold, dtype=jnp.int32)[:, None] * rows
    keys = (target + chunks).reshape(groups, top, 1, fold * per * tokens)
    on_wire = np.transpose(
        np.arange(fold * rows, dtype=np.int32).reshape(fold, experts, block), (1, 0, 2)
    ).reshape(-1)
    spots = np.repeat(on_wire[:, None], fold * per * tokens, axis=1)
    pack = (on_wire[:, None] == np.arange(fold * rows)[None, :]).astype(np.float32)
    scales = jnp.transpose(
        gates[0].reshape(groups, per * tokens, top), (0, 2, 1)
    )[..., None]
    x_groups = x_saved[0].reshape(groups, per * tokens, width)
    if cotangent.shape[2] % 128:
        cotangent = lax.all_gather(cotangent, "section", axis=2, tiled=True)
    cot_groups = cotangent.reshape(groups, per * tokens, cotangent.shape[2])

    vmem = pl.BlockSpec(memory_space=pltpu.VMEM)
    slots = (groups, experts, fold * block, width // fold)
    whole = (2, groups, rows, width)
    dma = pltpu.SemaphoreType.DMA
    grad_w = jax.ShapeDtypeStruct((hidden, width), BF16)
    results = pl.pallas_call(
        functools.partial(relay_kernel, sections, experts, batches, groups, pair, fold),
        out_shape=(
            jax.ShapeDtypeStruct((groups, per * tokens, width), BF16), grad_w, grad_w, grad_w,
        ),
        in_specs=[vmem] * 7 + [pl.BlockSpec(memory_space=pl.ANY)] * 3,
        out_specs=(vmem,) * 4,
        scratch_shapes=[
            pltpu.VMEM((groups, per * tokens, width), BF16),
            pltpu.VMEM(slots, BF16),
            pltpu.VMEM(slots, BF16),
            pltpu.VMEM(whole, BF16),
            pltpu.VMEM(slots, BF16),
            pltpu.VMEM(slots, BF16),
            pltpu.VMEM(whole, BF16),
            pltpu.VMEM(slots, BF16),
            pltpu.VMEM(slots, BF16),
            pltpu.VMEM((4 * hidden, width), BF16),
            pltpu.VMEM((2 * hidden, width), BF16),
            pltpu.VMEM((2, groups, rows, 3 * hidden), BF16),
            pltpu.VMEM((groups, rows, 3 * hidden), BF16),
            pltpu.VMEM((3 * hidden, 2 * groups * rows), BF16),
            pltpu.VMEM((groups, rows, 2 * hidden), F32),
            pltpu.VMEM((groups, rows, 2 * hidden), F32),
        ]
        + [dma((groups, experts))] * 6
        + [dma((groups,)), dma((groups,)), dma((groups,)), dma((groups, sections))]
        + [dma((3,))] * 3
        + [dma((groups,))] * 6,
        compiler_params=pltpu.CompilerParams(
            collective_id=0, has_side_effects=True, vmem_limit_bytes=60 * 2**20
        ),
    )(
        x_groups, cot_groups, scales, keys, jnp.asarray(spots),
        jnp.asarray(pack.T, BF16), jnp.asarray(pack, BF16), w_gate[0], w_up[0], w_down[0]
    )
    grad_inputs = results[0].reshape(1, batches, tokens, width)
    return (grad_inputs, results[1][None], results[2][None], results[3][None])


def solution(mesh):
    rows = P("section", None, "expert", None)
    halves = P("section", "expert", None)
    return jax.shard_map(
        functools.partial(on_device, 12), mesh=mesh,
        in_specs=(rows, rows, rows, P(None, "expert", "section"), halves, halves, halves),
        out_specs=(rows, halves, halves, halves),
        check_vma=False,
    )
```

```python
import functools

import jax
import jax.numpy as jnp
import numpy as np
from jax import lax
from jax.experimental import pallas as pl
from jax.experimental.pallas import tpu as pltpu
from jax.sharding import PartitionSpec as P

SPLIT = 2
MESH = pl.DeviceIdType.MESH
F32 = jnp.float32
BF16 = jnp.bfloat16


def relay_kernel(
    sections, experts, batches, groups, pair, fold,
    x_ref, cot_ref, gates_ref, keys_ref, spots_ref, unpack_ref, pack_ref, wg_ref, wu_ref, wd_ref,
    out_ref, dwg_ref, dwu_ref, dwd_ref,
    up_buf, x_send, x_wire, x_rows, g_send, g_wire, g_rows, r_send, r_recv, w_gu, w_d, w_gut, w_dt, acts, acts_send, acts_t,
    slope_buf, swish_buf,
    x_ss, x_rs, g_ss, g_rs, r_ss, r_rs, hop_ss, hop_rs, top_ss, top_rs, w_ss, w_rs, w_ls,
    px_ss, px_rs, pg_ss, pg_rs, pa_ss, pa_rs,
):
    section = lax.axis_index("section")
    place_in = lax.axis_index("expert")
    chip = place_in // SPLIT
    core = place_in % SPLIT
    other = chip * SPLIT + (1 - core)
    last = section == sections - 1
    rows = x_rows.shape[2]
    width = x_ref.shape[2]
    chunk = width // fold
    wire = x_send.shape[1:]
    hidden = wg_ref.shape[0]
    piece = cot_ref.shape[2]
    gathered = piece == width

    def remote(src, dst, ss, rs, sec, exp):
        return pltpu.make_async_remote_copy(
            src_ref=src, dst_ref=dst, send_sem=ss, recv_sem=rs,
            device_id=(sec, exp), device_id_type=MESH,
        )

    def peer(step):
        return lax.rem(chip + step, experts)

    own_w = (wg_ref, wu_ref, wd_ref)
    own_at = [w_gu.at[pl.ds(0, hidden)], w_gu.at[pl.ds(hidden, hidden)], w_d.at[pl.ds(0, hidden)]]
    other_at = [
        w_gu.at[pl.ds(2 * hidden, hidden)], w_gu.at[pl.ds(3 * hidden, hidden)],
        w_d.at[pl.ds(hidden, hidden)],
    ]
    local_copies = [
        pltpu.make_async_copy(own_w[i], own_at[i], w_ls.at[i]) for i in range(3)
    ]
    for copy in local_copies:
        copy.start()

    barrier = pltpu.get_barrier_semaphore()
    for step in range(1, experts):
        pl.semaphore_signal(
            barrier, inc=1, device_id=(section, peer(step) * SPLIT + core), device_id_type=MESH
        )
    pl.semaphore_signal(barrier, inc=1, device_id=(section, other), device_id_type=MESH)
    for step in range(1, sections):
        pl.semaphore_signal(
            barrier, inc=1, device_id=(lax.rem(section + step, sections), place_in),
            device_id_type=MESH,
        )
    pl.semaphore_wait(barrier, experts - 1 + 1 + sections - 1)

    def exchange(send, recv, ss, rs, g, step):
        to = peer(step)
        return remote(
            send.at[g, to], recv.at[g, chip], ss.at[g, to], rs.at[g, chip],
            section, to * SPLIT + core,
        )

    def arrival(send, recv, ss, rs, g, step):
        source = peer(step)
        return remote(
            send.at[g, source], recv.at[g, source], ss.at[g, source], rs.at[g, source],
            section, source * SPLIT + core,
        )

    def send_all(send, recv, ss, rs, g):
        for step in range(1, experts):
            exchange(send, recv, ss, rs, g, step).start()

    def wait_all(send, recv, ss, rs, g):
        for step in range(1, experts):
            arrival(send, recv, ss, rs, g, step).wait_recv()

    def wait_sent(send, recv, ss, rs, g):
        for step in range(1, experts):
            exchange(send, recv, ss, rs, g, step).wait_send()

    def top_copy(g):
        return remote(
            cot_ref.at[g], up_buf.at[g, :, pl.ds(pl.multiple_of(section * piece, 128), piece)],
            top_ss.at[g], top_rs.at[g, section], sections - 1, place_in,
        )

    def hop_copy(g):
        return remote(
            out_ref.at[g], up_buf.at[g], hop_ss.at[g], hop_rs.at[g],
            jnp.maximum(section - 1, 0), place_in,
        )

    def one_hot(g, k):
        return jnp.where(spots_ref[...] == keys_ref[g, k], 1.0, 0.0).astype(BF16)

    def both_hot(g):
        hot = one_hot(g, 0)
        for k in range(1, keys_ref.shape[1]):
            hot = hot + one_hot(g, k)
        return hot

    def stacked(value):
        return jnp.concatenate(
            [value[:, c * chunk : (c + 1) * chunk] for c in range(fold)], axis=0
        )

    def side_by_side(value, count):
        return jnp.concatenate(
            [value[c * count : (c + 1) * count] for c in range(fold)], axis=1
        )

    def unpacked(buf, g):
        return side_by_side(
            jnp.dot(
                unpack_ref[...], buf[g].reshape(fold * rows, chunk), preferred_element_type=F32
            ).astype(BF16),
            rows,
        )

    def to_partner(buf, ss, rs, g):
        return remote(buf.at[0, g], buf.at[1, g], ss.at[g], rs.at[g], section, other)

    def acts_copy(g):
        return remote(
            acts_send.at[g], acts.at[1, g], pa_ss.at[g], pa_rs.at[g], section, other
        )

    weight_copies = [
        remote(own_w[i], other_at[i], w_ss.at[i], w_rs.at[i], section, other) for i in range(3)
    ]

    ahead = jnp.where(last, min(pair, groups), groups)
    for copy in weight_copies:
        copy.start()

    def place_inputs(g):
        placed = jnp.dot(both_hot(g), stacked(x_ref[g]), preferred_element_type=F32)
        x_send[g] = placed.astype(BF16).reshape(wire)
        x_wire[g, chip] = x_send[g, chip]

    if not gathered:
        @pl.when(jnp.logical_not(last))
        def _():
            @pl.loop(0, groups)
            def _(g):
                top_copy(g).start()

    @pl.loop(0, ahead)
    def _(g):
        place_inputs(g)
        send_all(x_send, x_wire, x_ss, x_rs, g)

    def rows_arrived(g):
        wait_all(x_send, x_wire, x_ss, x_rs, g)
        x_rows[0, g] = unpacked(x_wire, g)
        to_partner(x_rows, px_ss, px_rs, g).start()

    def forward(p):
        first = p * pair
        for i in range(pair):
            rows_arrived(first + i)
        members = pl.ds(first, pair)
        rows_in = x_rows[0, members].reshape(pair * rows, width)
        for half in range(2):
            both = jnp.dot(
                rows_in, w_gut[:, pl.ds(half * 2 * hidden, 2 * hidden)],
                preferred_element_type=F32,
            )
            pre_gate, pre_up = both[:, :hidden], both[:, hidden:]
            sigmoid = jax.nn.sigmoid(pre_gate)
            swished = pre_gate * sigmoid
            slope = pre_up * (sigmoid * (1.0 + pre_gate * (1.0 - sigmoid)))
            act = (swished * pre_up).astype(BF16)
            columns = pl.ds(half * hidden, hidden)
            swish_buf[members, :, columns] = swished.reshape(pair, rows, hidden)
            slope_buf[members, :, columns] = slope.reshape(pair, rows, hidden)
            third = pl.ds(2 * hidden, hidden)
            if half == 0:
                acts[0, members, :, third] = act.reshape(pair, rows, hidden)
            else:
                acts_send[members, :, third] = act.reshape(pair, rows, hidden)

    def dispatch(g):
        @pl.when(last)
        def _():
            if gathered:
                up_buf[g] = cot_ref[g]
            else:
                for z in range(sections - 1):
                    remote(
                        cot_ref.at[g], up_buf.at[g, :, pl.ds(z * piece, piece)],
                        top_ss.at[g], top_rs.at[g, z], section, place_in,
                    ).wait_recv()
                up_buf[g, :, pl.ds((sections - 1) * piece, piece)] = cot_ref[g]

        @pl.when(jnp.logical_not(last))
        def _():
            hop_copy(g).wait_recv()

        upstream = up_buf[g].astype(F32)
        placed = jnp.zeros((fold * rows, chunk), F32)
        for k in range(gates_ref.shape[1]):
            scaled = (upstream * gates_ref[g, k]).astype(BF16)
            placed += jnp.dot(one_hot(g, k), stacked(scaled), preferred_element_type=F32)
        g_send[g] = placed.astype(BF16).reshape(wire)
        send_all(g_send, g_wire, g_ss, g_rs, g)
        g_wire[g, chip] = g_send[g, chip]

    def backward(g):
        wait_all(g_send, g_wire, g_ss, g_rs, g)

        @pl.when(jnp.logical_and(last, g + pair < groups))
        def _():
            send_all(x_send, x_wire, x_ss, x_rs, g + pair)

        rows_grad = unpacked(g_wire, g)
        g_rows[0, g] = rows_grad
        d_hidden = jnp.dot(rows_grad, w_dt[...], preferred_element_type=F32)
        d_gate = (d_hidden * slope_buf[g]).astype(BF16)
        d_up = (d_hidden * swish_buf[g]).astype(BF16)
        slopes = jnp.concatenate(
            [d_gate[:, :hidden], d_up[:, :hidden], d_gate[:, hidden:], d_up[:, hidden:]], axis=1
        )
        acts[0, g, :, pl.ds(0, 2 * hidden)] = slopes[:, : 2 * hidden]
        acts_send[g, :, pl.ds(0, 2 * hidden)] = slopes[:, 2 * hidden :]

        half = width // 2
        total = jnp.concatenate(
            [
                jnp.dot(
                    slopes, w_gu[:, pl.ds(i * half, half)], preferred_element_type=F32
                ).astype(BF16)
                for i in range(2)
            ],
            axis=1,
        )
        packed = jnp.dot(pack_ref[...], stacked(total), preferred_element_type=F32)
        r_send[g] = packed.astype(BF16).reshape(wire)
        send_all(r_send, r_recv, r_ss, r_rs, g)
        r_recv[g, chip] = r_send[g, chip]
        to_partner(g_rows, pg_ss, pg_rs, g).start()
        acts_copy(g).start()

    def combine(g):
        wait_all(r_send, r_recv, r_ss, r_rs, g)
        picked = lax.dot_general(
            both_hot(g), r_recv[g].reshape(fold * rows, chunk), (((0,), (0,)), ((), ())),
            preferred_element_type=F32,
        )
        back = side_by_side(picked, x_ref.shape[1])
        out_ref[g] = (up_buf[g].astype(F32) + back).astype(BF16)

        @pl.when(section > 0)
        def _():
            hop_copy(g).start()

    def turn(source, result, first, count):
        @pl.loop(0, width // 256)
        def _(t):
            span = pl.ds(pl.multiple_of(t * 256, 256), 256)
            result[span, pl.ds(first, count)] = source[pl.ds(first, count), span].T

    def wait_weights(first, end):
        for i in range(first, end):
            local_copies[i].wait()
        if first == 0:
            turn(w_gu, w_gut, 0, 2 * hidden)
        else:
            turn(w_d, w_dt, 0, hidden)
        for i in range(first, end):
            weight_copies[i].wait_recv()
        if first == 0:
            turn(w_gu, w_gut, 2 * hidden, 2 * hidden)
        else:
            turn(w_d, w_dt, hidden, hidden)

    pairs = groups // pair
    upfront = jnp.where(last, 0, jnp.minimum(sections - section, pairs))

    @pl.when(jnp.logical_not(last))
    def _():
        wait_weights(0, 2)

        @pl.loop(0, upfront)
        def _(p):
            forward(p)

    @pl.loop(0, groups + 1)
    def _(g):
        @pl.when(g < groups)
        def _():
            dispatch(g)

        @pl.when(jnp.logical_and(last, g + pair < groups))
        def _():
            place_inputs(g + pair)

        @pl.when(jnp.logical_and(last, g == 0))
        def _():
            wait_weights(0, 2)

        @pl.when(jnp.logical_and(g // pair + upfront < pairs, lax.rem(g, pair) == 0))
        def _():
            forward(g // pair + upfront)

        @pl.when(g == 0)
        def _():
            wait_weights(2, 3)

        @pl.when(g > 0)
        def _():
            combine(g - 1)

        @pl.when(g < groups)
        def _():
            backward(g)

    @pl.loop(0, groups)
    def _(g):
        to_partner(x_rows, px_ss, px_rs, g).wait_recv()
        to_partner(g_rows, pg_ss, pg_rs, g).wait_recv()
        acts_copy(g).wait_recv()

    total_rows = 2 * groups * rows
    for i in range(3):
        acts_t[pl.ds(i * hidden, hidden), :] = (
            acts[:, :, :, pl.ds(i * hidden, hidden)].reshape(total_rows, hidden).T
        )
    share = 1.0 / batches

    @pl.loop(0, width // 256)
    def _(t):
        columns = pl.ds(pl.multiple_of(t * 256, 128), 256)
        rows_in = x_rows[:, :, :, columns].reshape(total_rows, 256)
        rows_grad = g_rows[:, :, :, columns].reshape(total_rows, 256)
        for i, (result, side) in enumerate(
            ((dwg_ref, rows_in), (dwu_ref, rows_in), (dwd_ref, rows_grad))
        ):
            grad = jnp.dot(
                acts_t[pl.ds(i * hidden, hidden), :], side, preferred_element_type=F32
            )
            result[:, columns] = (grad * share).astype(BF16)

    @pl.loop(0, groups)
    def _(g):
        wait_sent(x_send, x_wire, x_ss, x_rs, g)
        wait_sent(g_send, g_wire, g_ss, g_rs, g)
        wait_sent(r_send, r_recv, r_ss, r_rs, g)
        to_partner(x_rows, px_ss, px_rs, g).wait_send()
        to_partner(g_rows, pg_ss, pg_rs, g).wait_send()
        acts_copy(g).wait_send()

        @pl.when(section > 0)
        def _():
            hop_copy(g).wait_send()

        if not gathered:
            @pl.when(jnp.logical_not(last))
            def _():
                top_copy(g).wait_send()

    for copy in weight_copies:
        copy.wait_send()


def on_device(group_rows, x_saved, routes, gates, cotangent, w_gate, w_up, w_down):
    sections = lax.axis_size("section")
    experts = lax.axis_size("expert") // SPLIT
    batches, tokens, width = x_saved.shape[1:]
    top = routes.shape[3]
    hidden = w_gate.shape[1]
    capacity = max(2, 3 * tokens * top // (2 * experts))
    per = 1
    while per * capacity < group_rows and batches % (2 * per) == 0:
        per *= 2
    groups = batches // per
    block = per * capacity
    fold = 0
    for parts in (4, 2, 1):
        if block * parts % 16 == 0 and experts * block % 16 == 0 and width % (128 * parts) == 0:
            fold = parts
    if fold == 0:
        fold, block = 1, -(-block // 16) * 16
    rows = experts * block
    pair = 2 if groups % 2 == 0 and rows <= 128 else 1

    flat = routes[0].reshape(batches, tokens * top)
    hot = (flat[:, :, None] == jnp.arange(experts, dtype=jnp.int32)).astype(jnp.int32)
    earlier = jnp.cumsum(hot, axis=1) - hot
    within = jnp.sum(earlier * hot, axis=2)
    batch_in = jnp.arange(batches, dtype=jnp.int32)[:, None] % per
    target = (flat * block + batch_in * capacity + within).reshape(groups, per, tokens, top)
    target = jnp.transpose(target, (0, 3, 1, 2)).reshape(groups, top, 1, per * tokens)
    chunks = jnp.arange(fold, dtype=jnp.int32)[:, None] * rows
    keys = (target + chunks).reshape(groups, top, 1, fold * per * tokens)
    on_wire = np.transpose(
        np.arange(fold * rows, dtype=np.int32).reshape(fold, experts, block), (1, 0, 2)
    ).reshape(-1)
    spots = np.repeat(on_wire[:, None], fold * per * tokens, axis=1)
    pack = (on_wire[:, None] == np.arange(fold * rows)[None, :]).astype(np.float32)
    scales = jnp.transpose(
        gates[0].reshape(groups, per * tokens, top), (0, 2, 1)
    )[..., None]
    x_groups = x_saved[0].reshape(groups, per * tokens, width)
    if cotangent.shape[2] % 128:
        cotangent = lax.all_gather(cotangent, "section", axis=2, tiled=True)
    cot_groups = cotangent.reshape(groups, per * tokens, cotangent.shape[2])

    vmem = pl.BlockSpec(memory_space=pltpu.VMEM)
    slots = (groups, experts, fold * block, width // fold)
    whole = (2, groups, rows, width)
    dma = pltpu.SemaphoreType.DMA
    grad_w = jax.ShapeDtypeStruct((hidden, width), BF16)
    results = pl.pallas_call(
        functools.partial(relay_kernel, sections, experts, batches, groups, pair, fold),
        out_shape=(
            jax.ShapeDtypeStruct((groups, per * tokens, width), BF16), grad_w, grad_w, grad_w,
        ),
        in_specs=[vmem] * 7 + [pl.BlockSpec(memory_space=pl.ANY)] * 3,
        out_specs=(vmem,) * 4,
        scratch_shapes=[
            pltpu.VMEM((groups, per * tokens, width), BF16),
            pltpu.VMEM(slots, BF16),
            pltpu.VMEM(slots, BF16),
            pltpu.VMEM(whole, BF16),
            pltpu.VMEM(slots, BF16),
            pltpu.VMEM(slots, BF16),
            pltpu.VMEM(whole, BF16),
            pltpu.VMEM(slots, BF16),
            pltpu.VMEM(slots, BF16),
            pltpu.VMEM((4 * hidden, width), BF16),
            pltpu.VMEM((2 * hidden, width), BF16),
            pltpu.VMEM((width, 4 * hidden), BF16),
            pltpu.VMEM((width, 2 * hidden), BF16),
            pltpu.VMEM((2, groups, rows, 3 * hidden), BF16),
            pltpu.VMEM((groups, rows, 3 * hidden), BF16),
            pltpu.VMEM((3 * hidden, 2 * groups * rows), BF16),
            pltpu.VMEM((groups, rows, 2 * hidden), F32),
            pltpu.VMEM((groups, rows, 2 * hidden), F32),
        ]
        + [dma((groups, experts))] * 6
        + [dma((groups,)), dma((groups,)), dma((groups,)), dma((groups, sections))]
        + [dma((3,))] * 3
        + [dma((groups,))] * 6,
        compiler_params=pltpu.CompilerParams(
            collective_id=0, has_side_effects=True, vmem_limit_bytes=62 * 2**20
        ),
    )(
        x_groups, cot_groups, scales, keys, jnp.asarray(spots),
        jnp.asarray(pack.T, BF16), jnp.asarray(pack, BF16), w_gate[0], w_up[0], w_down[0]
    )
    grad_inputs = results[0].reshape(1, batches, tokens, width)
    return (grad_inputs, results[1][None], results[2][None], results[3][None])


def solution(mesh):
    rows = P("section", None, "expert", None)
    halves = P("section", "expert", None)
    return jax.shard_map(
        functools.partial(on_device, 12), mesh=mesh,
        in_specs=(rows, rows, rows, P(None, "expert", "section"), halves, halves, halves),
        out_specs=(rows, halves, halves, halves),
        check_vma=False,
    )
```
